256 devices in a mesh: row: 8 (over y_hi, x), col: 16 (over y_lo, z), pts: 2 (over core).
Axes of the slice: x: 4, y: 4 (y_hi: 2, y_lo: 2; y = y_hi * 2 + y_lo), z: 8, core: 2. Of those that a mesh axis runs over, the one named last changes fastest.
Arguments:
- green_panel: bfloat16 [4, 2, 512, 6144], P(None, None, 'col', 'pts'), may hold values from -6 to 6
- log_psd: float32 [2, 4, 3072], P('pts', None, ('row', 'col')), may hold values from -1.1 to 1.1
- observed: float32 [4, 2, 512, 512], P(None, None, 'row', 'col'), may hold values from -1 to 1
- pair_weights: int32 [512, 512], P('row', 'col'), may hold values from 0 to 4, as said below
Outputs:
- updated_log_psd: float32 [2, 4, 3072], P('pts', None, ('row', 'col'))
The draws below stay inside these ranges and needn't reach their ends.
Inputs may be any that keep to these rules, and one draw needn't show every extreme that they name: pair_weights is 0 for pairs that are not listed and for every station paired with itself; the share of listed pairs differs from one block of 64 x 32 pairs (one index of row by one of col) to another, and some such blocks list no pair.
All inputs are finite; a program needn't handle non-finite values.
Results may differ from the reference program's by a relative error of at most 0.0014.
Values may be sent and summed in bfloat16 or wider, within the bound.
A program may use at most 64 MiB of HBM per device.

```python
import jax
import jax.numpy as jnp
from jax import lax

NS = 512
F = 4
PT_DEV = 3072
ITERS = 2
PTS = 6144
GI = 64
GJ = 32
N_PTS = 2


def draw_pair_weights(key, part):
    key_list = jax.random.split(key, 5)
    row_blocks = NS // GI
    col_blocks = NS // GJ
    block_count = row_blocks * col_blocks
    block_level = jax.random.randint(key_list[0], (block_count,), 0, 4)
    empty_block = jax.random.randint(key_list[1], (), 0, block_count)
    full_block = (empty_block + 1 + jax.random.randint(key_list[2], (), 0, block_count - 1)) % block_count
    block_ids = jnp.arange(block_count)
    block_level = jnp.where(block_ids == empty_block, 0, jnp.where(block_ids == full_block, 3, block_level))
    block_share = jnp.array([0, 15, 40, 90], jnp.int32)[block_level].reshape(row_blocks, col_blocks)
    row_block = jnp.arange(NS) // GI
    col_block = jnp.arange(NS) // GJ
    pair_share = block_share[row_block][:, col_block]
    pick_draw = jax.random.randint(key_list[3], (NS, NS), 0, 100)
    pair_value = jax.random.randint(key_list[4], (NS, NS), 1, 5)
    self_pair = jnp.arange(NS)[:, None] == jnp.arange(NS)[None, :]
    chosen = jnp.logical_and(pick_draw < pair_share, jnp.logical_not(self_pair))
    return jnp.where(chosen, pair_value, 0).astype(jnp.int32)


def draw_log_psd(key, part):
    array_shape = (N_PTS, F, PT_DEV)
    position = (jnp.arange(N_PTS)[:, None, None] * PT_DEV + jnp.arange(PT_DEV)[None, None, :]).astype(jnp.float32)
    position = position / (N_PTS * PT_DEV)
    rough_part = 0.3 * jax.random.truncated_normal(key, -2.0, 2.0, array_shape, jnp.float32)
    return (rough_part + position - 0.5).astype(jnp.float32)


def draw_observed(key, part):
    array_shape = (F, 2, NS, NS)
    spread_scale = 1.7 * float(PTS) ** (-0.5)
    raw_values = jax.random.truncated_normal(key, -3.0, 3.0, array_shape, jnp.float32)
    return (spread_scale * raw_values).astype(jnp.float32)


def level_of(key, extent, pieces, low, largest):
    loudness = 1.0
    for axis_at, blocks in pieces:
        steps = jax.random.uniform(jax.random.fold_in(jax.random.fold_in(key, 6), axis_at), (blocks,), jnp.float32, low / len(pieces), largest / len(pieces))
        loudness = loudness * jnp.repeat(jnp.exp(steps), extent[axis_at] // blocks).reshape((-1,) + (1,) * (len(extent) - 1 - axis_at))
    return loudness


def normal_values(own_key, shape, spread, limit, pieces=(), kind=jnp.bfloat16):
    values = jax.random.normal(own_key, shape, jnp.float32) * spread
    if len(pieces) > 0:
        values = level_of(own_key, shape, pieces, -0.22, 0.18) * values
    return jnp.clip(values, min=-limit, max=limit).astype(kind)


def setup_inputs(seed: int = 0) -> dict:
    arg_keys = jax.random.split(jax.random.key(seed), 5)
    return {
        "green_panel": normal_values(arg_keys[0], (F, 2, NS, PTS), 1.0, 6.0, ((2, 16), (3, 2))),
        "log_psd": draw_log_psd(jax.random.fold_in(arg_keys[4], 71), 0),
        "observed": draw_observed(jax.random.fold_in(arg_keys[4], 71), 0),
        "pair_weights": draw_pair_weights(jax.random.fold_in(arg_keys[4], 71), 0),
    }


epsilon = 1e-06
descent = 0.1

def reference(green_panel, log_psd, observed, pair_weights):
    quad_weight = 1.0 / (N_PTS * PT_DEV)
    pair_scale = pair_weights.astype(jnp.float32)
    log_start = jnp.transpose(log_psd, (1, 0, 2)).reshape(F, N_PTS * PT_DEV)

    def run_sweep(sweep_idx, log_field):
        psd_field = jnp.exp(log_field)
        gradient_rows = []
        for channel in range(F):
            real_part = green_panel[channel, 0]
            imag_part = green_panel[channel, 1]
            weight_real = (real_part.astype(jnp.float32) * psd_field[channel][None, :]).astype(jnp.bfloat16)
            weight_imag = (imag_part.astype(jnp.float32) * psd_field[channel][None, :]).astype(jnp.bfloat16)
            corr_real = (jnp.dot(real_part, weight_real.T, preferred_element_type=jnp.float32) + jnp.dot(imag_part, weight_imag.T, preferred_element_type=jnp.float32)) * quad_weight
            corr_imag = (jnp.dot(imag_part, weight_real.T, preferred_element_type=jnp.float32) - jnp.dot(real_part, weight_imag.T, preferred_element_type=jnp.float32)) * quad_weight
            adj_real = (pair_scale * (corr_real - observed[channel, 0])).astype(jnp.bfloat16)
            adj_imag = (pair_scale * (corr_imag - observed[channel, 1])).astype(jnp.bfloat16)
            accum_real = jnp.dot(adj_real, real_part, preferred_element_type=jnp.float32) - jnp.dot(adj_imag, imag_part, preferred_element_type=jnp.float32)
            accum_imag = jnp.dot(adj_real, imag_part, preferred_element_type=jnp.float32) + jnp.dot(adj_imag, real_part, preferred_element_type=jnp.float32)
            inner_sum = lax.optimization_barrier(jnp.sum(real_part.astype(jnp.float32) * accum_real + imag_part.astype(jnp.float32) * accum_imag, axis=0))
            gradient_rows.append(quad_weight * psd_field[channel] * inner_sum)
        gradient = jnp.stack(gradient_rows)
        grad_scale = jnp.sqrt(jnp.mean(gradient * gradient) + epsilon)
        return log_field - descent * gradient / grad_scale
    log_final = lax.fori_loop(0, ITERS, run_sweep, log_start)
    return jnp.transpose(log_final.reshape(F, N_PTS, PT_DEV), (1, 0, 2))
```

```python
import functools

import jax
import jax.numpy as jnp
from jax import lax
from jax.experimental import pallas as pl
from jax.experimental.pallas import tpu as pltpu
from jax.sharding import PartitionSpec as P

MESH = pl.DeviceIdType.MESH
HIGHEST = lax.Precision.HIGHEST
F32 = jnp.float32
BF16 = jnp.bfloat16

ITERS = 2
NX = 4
NZ = 8
NO = 8
ST = 32
NP = 768
RUN = 24
ENTRIES = 4 * 6144
QUAD = 1.0 / 6144
EPSILON = 1e-06
DESCENT = 0.1

FIRST_J = (0, 1, 2)


def wait_bytes(ref, sem):
    pltpu.make_async_copy(ref, ref, sem).wait()


def kernel(
    green, logp, obs, weights, out,
    u, y, x_left, obs_v, w_v, msg, e_in, d_all, w_all,
    l_src, l_in, l_z, l_rows, c_part, rs, b_out, b_full, g_mine, g_all, s_mine, s_all, t_mine, t_all,
    m_mine, o_mine, m_in, o_in, rows_m, rows_g,
    in_sem, gr_sem, gs_sem, er_sem, es_sem, lr_sem, ls_sem, ls2_sem,
    ph_r, ph_s, mr_sem, ms_sem, or_sem, os_sem,
):
    row = lax.axis_index("row")
    col = lax.axis_index("col")
    core = lax.axis_index("pts")
    yh, x = row // 4, row % 4
    yl, z = col // 8, col % 8
    me = yh * 4 + yl * 2 + core
    other = 1 - yl

    def dev(x_, yh_, yl_, z_, core_):
        return (yh_ * 4 + x_, yl_ * 8 + z_, core_)

    def zdev(d):
        return dev(x, yh, yl, (z + d) % NZ, core)

    def odev(d):
        o = (me + d) % NO
        return o, dev(x, o // 4, (o // 2) % 2, z, o % 2)

    def xdev(d):
        return dev((x + d) % NX, yh, yl, z, core)

    def is_me(dest):
        return jnp.logical_and(jnp.logical_and(dest[0] == row, dest[1] == col), dest[2] == core)

    obs_copy = pltpu.make_async_copy(obs, obs_v, in_sem.at[0])
    w_copy = pltpu.make_async_copy(weights, w_v, in_sem.at[1])
    obs_copy.start()
    w_copy.start()

    def panel(comp, lo):
        start = pl.multiple_of((yh * 2 + lo) * NP, 128)
        return green.at[x, comp, :, pl.ds(start, NP)]

    for comp in range(2):
        pltpu.make_async_copy(panel(comp, yl), u.at[yl, 0, 0, :, pl.ds(comp * NP, NP)], in_sem.at[2]).start()

    def centre(zi, zj):
        delta = (zj - zi) % NZ
        from_i = jnp.where(delta >= 4, 2, jnp.where(delta >= 2, 1, 0))
        from_j = jnp.where(delta == 7, 0, 1)
        zc = jnp.where(delta <= 4, zi + from_i, zj + from_j) % NZ
        return delta, zc

    def pair_dest(plane, zl):
        delta, zc = centre(2 * x + zl, z)
        swap = delta >= 5
        return delta, dev(plane, jnp.where(swap, yl, yh), jnp.where(swap, yh, yl), zc, core)

    pair_dests = []
    for plane in range(NX):
        for zl in range(2):
            pair_dests.append((plane, zl) + pair_dest(plane, zl))
    offsets = ((0, 0), (0, 1), (-1, 1), (-1, 2), (-2, 2), (2, -1), (1, -1), (1, 0))
    pair_sources = []
    for delta in range(NZ):
        zi, zj = (z + offsets[delta][0]) % NZ, (z + offsets[delta][1]) % NZ
        if delta <= 4:
            pair_sources.append(dev(zi // 2, yh, yl, zj, core))
        else:
            pair_sources.append(dev(zi // 2, yl, yh, zj, core))

    up = [dev(plane, yh, x // 2, z, core) for plane in range(NX)]
    down = [dev(2 * yl + k // 2, yh, k % 2, z, core) for k in range(4)]

    barrier = pltpu.get_barrier_semaphore()
    expected = jnp.int32(7 + 7 + 3 + 16)
    for d in range(1, NZ):
        pl.semaphore_signal(barrier, inc=1, device_id=zdev(d), device_id_type=MESH)
    for d in range(1, NO):
        pl.semaphore_signal(barrier, inc=1, device_id=odev(d)[1], device_id_type=MESH)
    for d in range(1, NX):
        pl.semaphore_signal(barrier, inc=1, device_id=xdev(d), device_id_type=MESH)
    for dest in pair_sources + up + down:
        @pl.when(jnp.logical_not(is_me(dest)))
        def _(dest=dest):
            pl.semaphore_signal(barrier, inc=1, device_id=dest, device_id_type=MESH)
    for dest in [entry[3] for entry in pair_dests] + up + down:
        expected = expected - is_me(dest).astype(jnp.int32)
    pl.semaphore_wait(barrier, expected)

    def send(src, dst, s_sem, r_sem, dest):
        copy = pltpu.make_async_remote_copy(
            src_ref=src, dst_ref=dst, send_sem=s_sem, recv_sem=r_sem, device_id=dest, device_id_type=MESH
        )
        copy.start()
        return copy

    partner = dev(x, yh, other, z, core)
    lane = lambda comp: pl.ds(comp * NP, NP)
    for comp in range(2):
        send(panel(comp, other), u.at[yl, 0, 0, :, lane(comp)], gs_sem.at[0], gr_sem.at[0], partner)
    for comp in range(2):
        send(panel(comp, yl), x_left.at[1, yl, :, lane(comp)], gs_sem.at[1], gr_sem.at[1], zdev(1))
        send(panel(comp, yl), u.at[yl, 1, 0, :, lane(comp)], gs_sem.at[2], gr_sem.at[2], zdev(-1))

    def send_or_keep(src, dst, s_sem, r_sem, dest):
        mine = is_me(dest)
        @pl.when(jnp.logical_not(mine))
        def _():
            send(src, dst, s_sem, r_sem, dest)
        @pl.when(mine)
        def _():
            pltpu.make_async_copy(src, dst, r_sem).start()

    def finish_send(src, s_sem, dest):
        @pl.when(jnp.logical_not(is_me(dest)))
        def _():
            wait_bytes(src, s_sem)

    slot = (x % 2) * 2 + yl
    l_src[...] = jnp.zeros_like(l_src)
    for f in range(NX):
        l_src[f, :, 0:RUN] = logp[0, f : f + 1, :]
    for f in range(NX):
        send_or_keep(l_src.at[f], l_in.at[slot], ls_sem.at[f], lr_sem.at[0], up[f])

    obs_copy.wait()
    w_copy.wait()
    for zl in range(2):
        w = w_v[zl * ST : (zl + 1) * ST, :].astype(F32)
        for f in range(NX):
            real = w * obs_v[f, 0, zl * ST : (zl + 1) * ST, :]
            imag = w * obs_v[f, 1, zl * ST : (zl + 1) * ST, :]
            msg[f, zl] = jnp.concatenate([real, imag, w, w], axis=1)

    wait_bytes(l_in, lr_sem.at[0])
    for d in range(1, NZ):
        send(l_in, l_z.at[z], ls2_sem.at[0], lr_sem.at[1], zdev(d))
    l_z[z] = l_in[...]

    for k, (plane, zl, delta, dest) in enumerate(pair_dests):
        send_or_keep(msg.at[plane, zl], e_in.at[delta], es_sem.at[k], er_sem.at[0], dest)

    wait_bytes(u.at[other, 0, 0], gr_sem.at[0])
    send(u.at[other, 0, 0], x_left.at[1, other], gs_sem.at[3], gr_sem.at[3], zdev(1))
    send(u.at[other, 0, 0], u.at[other, 1, 0], gs_sem.at[4], gr_sem.at[4], zdev(-1))

    wait_bytes(l_z.at[pl.ds(0, NZ - 1)], lr_sem.at[1])
    for zz in range(NZ):
        for k in range(4):
            l_rows[k * NZ + zz : k * NZ + zz + 1, :] = l_z[zz, k]
    point = lax.broadcasted_iota(jnp.int32, (128, NP), 1)
    run_of = lax.shift_right_logical(point * 2731, 16)
    spread = (point - run_of * RUN == lax.broadcasted_iota(jnp.int32, (128, NP), 0)).astype(F32)
    spread_rows = jnp.dot(l_rows[...], spread, precision=HIGHEST, preferred_element_type=F32)
    run_row = lax.shift_right_logical(lax.broadcasted_iota(jnp.int32, (32, NP), 1) * 2731, 16)
    log_field = jnp.sum(
        jnp.where(run_row == lax.broadcasted_iota(jnp.int32, (32, NP), 0), spread_rows, 0.0), axis=0, keepdims=True
    )

    def build_turned(lo, j):
        u[lo, j, 1, :, 0:NP] = -u[lo, j, 0, :, NP : 2 * NP]
        u[lo, j, 1, :, NP : 2 * NP] = u[lo, j, 0, :, 0:NP]

    def build_weighted(j, psd2):
        for lo in range(2):
            for turn in range(2):
                y[lo, j, turn] = (u[lo, j, turn].astype(F32) * psd2).astype(BF16)

    def correlate(g):
        count = 2 if g < 2 else 1
        left = x_left[g].reshape(2 * ST, 2 * NP)
        for lo in range(2):
            right = y[lo, FIRST_J[g] : FIRST_J[g] + count].reshape(count * 2 * ST, 2 * NP)
            product = lax.dot_general(left, right, (((1,), (1,)), ((), ())), preferred_element_type=F32)
            if count == 1:
                product = jnp.concatenate([product, jnp.zeros_like(product)], axis=1)
            c_part[lo, g] = product.reshape(2, 2, 16, 128).astype(BF16)

    psd = jnp.exp(log_field)
    psd2 = jnp.concatenate([psd, psd], axis=1)

    wait_bytes(u.at[yl, 0, 0], in_sem.at[2])
    for lo in range(2):
        x_left[0, lo] = u[lo, 0, 0]
        build_turned(lo, 0)
    build_weighted(0, psd2)

    for half, at in ((yl, 1), (other, 3)):
        wait_bytes(x_left.at[1, half], gr_sem.at[at])
        send(x_left.at[1, half], x_left.at[2, half], gs_sem.at[at + 4], gr_sem.at[at + 4], zdev(1))
        wait_bytes(u.at[half, 1, 0], gr_sem.at[at + 1])
        send(u.at[half, 1, 0], u.at[half, 2, 0], gs_sem.at[at + 5], gr_sem.at[at + 5], zdev(-1))
    for lo in range(2):
        build_turned(lo, 1)
    build_weighted(1, psd2)
    correlate(0)

    wait_bytes(e_in, er_sem.at[0])
    lane_at = lax.broadcasted_iota(jnp.int32, (ST, 128), 1)
    same = (lane_at % ST == lax.broadcasted_iota(jnp.int32, (ST, 128), 0)).astype(F32)
    part_at = lane_at // ST

    def turned(block):
        full = lax.dot_general(block, same, (((0,), (0,)), ((), ())), precision=HIGHEST, preferred_element_type=F32)
        result = jnp.where(part_at == 0, full[0:ST], 0.0)
        result = jnp.where(part_at == 1, -full[ST : 2 * ST], result)
        result = jnp.where(part_at == 2, full[2 * ST : 3 * ST], result)
        return jnp.where(part_at == 3, full[3 * ST : 4 * ST], result)

    none = jnp.zeros((ST, 128), F32)
    slots = (
        (e_in[0], e_in[1] + turned(e_in[7])),
        (e_in[2] + turned(e_in[6]), e_in[3] + turned(e_in[5])),
        (e_in[4], none),
    )
    low = lane_at < 2 * ST
    for g, (first, second) in enumerate(slots):
        d_all[g] = jnp.where(low, first, pltpu.roll(second, 64, 1))
        w_all[g] = jnp.where(low, pltpu.roll(first, 64, 1), second) * QUAD

    for half, at in ((yl, 5), (other, 7)):
        wait_bytes(x_left.at[2, half], gr_sem.at[at])
        wait_bytes(u.at[half, 2, 0], gr_sem.at[at + 1])
    for lo in range(2):
        build_turned(lo, 2)
    build_weighted(2, psd2)
    correlate(1)
    correlate(2)

    def exchange_rest(it, psd):
        phase = lambda k: (ph_s.at[it, k], ph_r.at[it, k])
        s_sem, r_sem = phase(0)
        for d in range(1, NO):
            o, dest = odev(d)
            send(c_part.at[(o // 2) % 2, :, o // 4, o % 2], rs.at[it, d - 1], s_sem, r_sem, dest)
        total = c_part[yl, :, yh, core].astype(F32)
        wait_bytes(rs.at[it], r_sem)
        for d in range(NO - 1):
            total = total + rs[it, d].astype(F32)
        own_rows = pl.ds(pl.multiple_of(core * 16, 16), 16)
        b_out[it] = (w_all[:, own_rows, :] * total - d_all[:, own_rows, :]).astype(BF16)
        s_sem, r_sem = phase(1)
        for d in range(1, NO):
            send(b_out.at[it], b_full.at[it, yl, :, yh, core], s_sem, r_sem, odev(d)[1])
        b_full[it, yl, :, yh, core] = b_out[it]
        wait_bytes(rs.at[it], r_sem)

        width = 384
        terms = []
        for c in range(2 * NP // width):
            lanes = slice(c * width, (c + 1) * width)
            term = jnp.zeros((1, width), F32)
            for g in range(3):
                count = 2 if g < 2 else 1
                field = jnp.zeros((2 * ST, width), F32)
                for lo in range(2):
                    b = b_full[it, lo, g].reshape(2 * ST, 128)[:, 0 : count * 2 * ST]
                    right = u[lo, FIRST_J[g] : FIRST_J[g] + count, :, :, lanes].reshape(count * 2 * ST, width)
                    field = field + jnp.dot(b, right, preferred_element_type=F32)
                left = x_left[g, :, :, lanes].reshape(2 * ST, width).astype(F32)
                term = term + jnp.sum(left * field, axis=0, keepdims=True)
            terms.append(term)
        half = len(terms) // 2
        mine = jnp.concatenate([terms[k] + terms[half + k] for k in range(half)], axis=1)
        g_mine[it] = mine
        s_sem, r_sem = phase(2)
        for d in range(1, NZ):
            send(g_mine.at[it], g_all.at[it, z], s_sem, r_sem, zdev(d))
        g_all[it, z] = mine
        wait_bytes(g_all.at[it, pl.ds(0, NZ - 1)], r_sem)
        summed = g_all[it, 0]
        for k in range(1, NZ):
            summed = summed + g_all[it, k]
        return QUAD * psd * summed

    def root_mean(it, gradient):
        phase = lambda k: (ph_s.at[it, k], ph_r.at[it, k])
        squares = jnp.broadcast_to(jnp.sum(gradient * gradient, axis=1, keepdims=True), (1, 128))
        s_mine[it] = squares
        s_sem, r_sem = phase(3)
        for d in range(1, NO):
            send(s_mine.at[it], s_all.at[it, me], s_sem, r_sem, odev(d)[1])
        s_all[it, me] = squares
        wait_bytes(s_all.at[it, pl.ds(0, NO - 1)], r_sem)
        total = s_all[it, 0]
        for k in range(1, NO):
            total = total + s_all[it, k]
        t_mine[it] = total
        s_sem, r_sem = phase(4)
        for d in range(1, NX):
            send(t_mine.at[it], t_all.at[it, x], s_sem, r_sem, xdev(d))
        t_all[it, x] = total
        wait_bytes(t_all.at[it, pl.ds(0, NX - 1)], r_sem)
        total = t_all[it, 0]
        for k in range(1, NX):
            total = total + t_all[it, k]
        return jnp.sqrt(total / ENTRIES + EPSILON)[:, 0:1]

    gradient = exchange_rest(0, psd)
    log_field = log_field - DESCENT * gradient / root_mean(0, gradient)

    psd = jnp.exp(log_field)
    psd2 = jnp.concatenate([psd, psd], axis=1)
    for j in range(3):
        build_weighted(j, psd2)
    for g in range(3):
        correlate_wait = g == 0
        if correlate_wait:
            wait_bytes(rs.at[0], ph_s.at[0, 0])
        correlate(g)
    m_mine[...] = log_field
    for k in range(4):
        send_or_keep(m_mine, m_in.at[x], ms_sem.at[k], mr_sem.at[0], down[k])
    gradient = exchange_rest(1, psd)
    o_mine[...] = gradient
    for k in range(4):
        send_or_keep(o_mine, o_in.at[x], os_sem.at[k], or_sem.at[0], down[k])
    scale = root_mean(1, gradient)

    wait_bytes(m_in, mr_sem.at[0])
    wait_bytes(o_in, or_sem.at[0])
    rows_m[...] = jnp.zeros_like(rows_m)
    for f in range(NX):
        rows_m[f : f + 1, :] = m_in[f] - DESCENT * o_in[f] / scale
    start = (slot * NZ + z) * RUN
    pick = (
        lax.broadcasted_iota(jnp.int32, (NP, 128), 0) == lax.broadcasted_iota(jnp.int32, (NP, 128), 1) + start
    ).astype(F32)
    picked = jnp.dot(rows_m[...], pick, precision=HIGHEST, preferred_element_type=F32)
    out[0] = picked[0:NX, 0:RUN]

    for k in range(9):
        wait_bytes(x_left.at[1, 0], gs_sem.at[k])
    for f in range(NX):
        finish_send(l_src.at[f], ls_sem.at[f], up[f])
    wait_bytes(l_z.at[pl.ds(0, NZ - 1)], ls2_sem.at[0])
    for k, (plane, zl, delta, dest) in enumerate(pair_dests):
        finish_send(msg.at[plane, zl], es_sem.at[k], dest)
    for it in range(ITERS):
        if it > 0:
            wait_bytes(rs.at[it], ph_s.at[it, 0])
        wait_bytes(rs.at[it], ph_s.at[it, 1])
        wait_bytes(g_all.at[it, pl.ds(0, NZ - 1)], ph_s.at[it, 2])
        wait_bytes(s_all.at[it, pl.ds(0, NO - 1)], ph_s.at[it, 3])
        wait_bytes(t_all.at[it, pl.ds(0, NX - 1)], ph_s.at[it, 4])
    for k in range(4):
        finish_send(m_mine, ms_sem.at[k], down[k])
        finish_send(o_mine, os_sem.at[k], down[k])


def body(green_panel, log_psd, observed, pair_weights):
    vmem = pltpu.VMEM
    dma = pltpu.SemaphoreType.DMA
    return pl.pallas_call(
        kernel,
        out_shape=jax.ShapeDtypeStruct(log_psd.shape, F32),
        in_specs=[
            pl.BlockSpec(memory_space=pl.ANY),
            pl.BlockSpec(memory_space=pltpu.VMEM),
            pl.BlockSpec(memory_space=pl.ANY),
            pl.BlockSpec(memory_space=pl.ANY),
        ],
        out_specs=pl.BlockSpec(memory_space=pltpu.VMEM),
        scratch_shapes=[
            vmem((2, 3, 2, ST, 2 * NP), BF16),
            vmem((2, 3, 2, ST, 2 * NP), BF16),
            vmem((3, 2, ST, 2 * NP), BF16),
            vmem((4, 2, 64, ST), F32),
            vmem((64, ST), jnp.int32),
            vmem((NX, 2, ST, 128), F32),
            vmem((NZ, ST, 128), F32),
            vmem((3, ST, 128), F32),
            vmem((3, ST, 128), F32),
            vmem((NX, 1, 128), F32),
            vmem((4, 1, 128), F32),
            vmem((NZ, 4, 1, 128), F32),
            vmem((32, 128), F32),
            vmem((2, 3, 2, 2, 16, 128), BF16),
            vmem((ITERS, NO - 1, 3, 16, 128), BF16),
            vmem((ITERS, 3, 16, 128), BF16),
            vmem((ITERS, 2, 3, 2, 2, 16, 128), BF16),
            vmem((ITERS, 1, NP), F32),
            vmem((ITERS, NZ, 1, NP), F32),
            vmem((ITERS, 1, 128), F32),
            vmem((ITERS, NO, 1, 128), F32),
            vmem((ITERS, 1, 128), F32),
            vmem((ITERS, NX, 1, 128), F32),
            vmem((1, NP), F32),
            vmem((1, NP), F32),
            vmem((NX, 1, NP), F32),
            vmem((NX, 1, NP), F32),
            vmem((8, NP), F32),
            vmem((8, NP), F32),
            dma((3,)),
            dma((9,)),
            dma((9,)),
            dma((1,)),
            dma((8,)),
            dma((2,)),
            dma((4,)),
            dma((1,)),
            dma((ITERS, 5)),
            dma((ITERS, 5)),
            dma((1,)),
            dma((4,)),
            dma((1,)),
            dma((4,)),
        ],
        compiler_params=pltpu.CompilerParams(
            collective_id=0, has_side_effects=True, vmem_limit_bytes=40 * 1024 * 1024
        ),
    )(green_panel, log_psd, observed, pair_weights)


def solution(mesh):
    return jax.shard_map(
        body,
        mesh=mesh,
        in_specs=(
            P(None, None, "col", "pts"),
            P("pts", None, ("row", "col")),
            P(None, None, "row", "col"),
            P("row", "col"),
        ),
        out_specs=P("pts", None, ("row", "col")),
        check_vma=False,
    )
```

```python
import functools

import jax
import jax.numpy as jnp
from jax import lax
from jax.experimental import pallas as pl
from jax.experimental.pallas import tpu as pltpu
from jax.sharding import PartitionSpec as P

MESH = pl.DeviceIdType.MESH
HIGHEST = lax.Precision.HIGHEST
F32 = jnp.float32
BF16 = jnp.bfloat16

ITERS = 2
NX = 4
NZ = 8
NO = 8
NS = NX * NO
ST = 32
NP = 768
RUN = 24
ENTRIES = 4 * 6144
QUAD = 1.0 / 6144
EPSILON = 1e-06
DESCENT = 0.1

FIRST_J = (0, 1, 2)


def wait_bytes(ref, sem):
    pltpu.make_async_copy(ref, ref, sem).wait()


def kernel(
    green, logp, obs, weights, out,
    u, x_left, x_psd, log_v, obs_v, w_v, msg, e_in, d_all, w_all,
    l_src, l_in, l_z, l_rows, c_part, rs, b_out, b_full, g_mine, g_all, s_mine, s_all,
    m_mine, o_mine, m_in, o_in, rows_m, rows_o,
    in_sem, gr_sem, gs_sem, er_sem, es_sem, lr_sem, ls_sem, ls2_sem,
    ph_r, ph_s, mr_sem, ms_sem, or_sem, os_sem,
):
    row = lax.axis_index("row")
    col = lax.axis_index("col")
    core = lax.axis_index("pts")
    yh, x = row // 4, row % 4
    yl, z = col // 8, col % 8
    me = yh * 4 + yl * 2 + core
    other = 1 - yl

    def dev(x_, yh_, yl_, z_, core_):
        return (yh_ * 4 + x_, yl_ * 8 + z_, core_)

    def zdev(d):
        return dev(x, yh, yl, (z + d) % NZ, core)

    def odev(d):
        o = (me + d) % NO
        return o, dev(x, o // 4, (o // 2) % 2, z, o % 2)

    def sdev(d):
        r = (x * NO + me + d) % NS
        return dev(r // NO, (r // 4) % 2, (r // 2) % 2, z, r % 2)

    def is_me(dest):
        return jnp.logical_and(jnp.logical_and(dest[0] == row, dest[1] == col), dest[2] == core)

    obs_copy = pltpu.make_async_copy(obs, obs_v, in_sem.at[0])
    w_copy = pltpu.make_async_copy(weights, w_v, in_sem.at[1])
    log_copy = pltpu.make_async_copy(logp, log_v, in_sem.at[3])
    log_copy.start()
    obs_copy.start()
    w_copy.start()

    def panel(comp, lo):
        start = pl.multiple_of((yh * 2 + lo) * NP, 128)
        return green.at[x, comp, :, pl.ds(start, NP)]

    for comp in range(2):
        pltpu.make_async_copy(panel(comp, yl), u.at[yl, 0, 0, :, pl.ds(comp * NP, NP)], in_sem.at[2]).start()

    def centre(zi, zj):
        delta = (zj - zi) % NZ
        from_i = jnp.where(delta >= 2, 1, 0)
        from_j = jnp.where(delta == 7, 0, jnp.where(delta == 4, 2, 1))
        zc = jnp.where(delta <= 3, zi + from_i, zj + from_j) % NZ
        return delta, zc

    def pair_dest(plane, zl):
        delta, zc = centre(2 * x + zl, z)
        swap = jnp.logical_or(delta == 0, delta >= 4)
        return delta, dev(plane, jnp.where(swap, yl, yh), jnp.where(swap, yh, yl), zc, core)

    pair_dests = []
    for plane in range(NX):
        for zl in range(2):
            pair_dests.append((plane, zl) + pair_dest(plane, zl))
    offsets = ((0, 0), (0, 1), (-1, 1), (-1, 2), (2, -2), (2, -1), (1, -1), (1, 0))
    pair_sources = []
    for delta in range(NZ):
        zi, zj = (z + offsets[delta][0]) % NZ, (z + offsets[delta][1]) % NZ
        if 1 <= delta <= 3:
            pair_sources.append(dev(zi // 2, yh, yl, zj, core))
        else:
            pair_sources.append(dev(zi // 2, yl, yh, zj, core))

    up = [dev(plane, yh, x // 2, z, core) for plane in range(NX)]
    down = [dev(2 * yl + k // 2, yh, k % 2, z, core) for k in range(4)]

    barrier = pltpu.get_barrier_semaphore()
    expected = jnp.int32(NZ - 1 + NS - 1 + 16)
    for d in range(1, NZ):
        pl.semaphore_signal(barrier, inc=1, device_id=zdev(d), device_id_type=MESH)
    for d in range(1, NS):
        pl.semaphore_signal(barrier, inc=1, device_id=sdev(d), device_id_type=MESH)
    for dest in pair_sources + up + down:
        @pl.when(jnp.logical_not(is_me(dest)))
        def _(dest=dest):
            pl.semaphore_signal(barrier, inc=1, device_id=dest, device_id_type=MESH)
    for dest in [entry[3] for entry in pair_dests] + up + down:
        expected = expected - is_me(dest).astype(jnp.int32)
    pl.semaphore_wait(barrier, expected)

    def send(src, dst, s_sem, r_sem, dest):
        copy = pltpu.make_async_remote_copy(
            src_ref=src, dst_ref=dst, send_sem=s_sem, recv_sem=r_sem, device_id=dest, device_id_type=MESH
        )
        copy.start()
        return copy

    partner = dev(x, yh, other, z, core)
    lane = lambda comp: pl.ds(comp * NP, NP)
    for comp in range(2):
        send(panel(comp, other), u.at[yl, 0, 0, :, lane(comp)], gs_sem.at[0], gr_sem.at[0], partner)
    for comp in range(2):
        send(panel(comp, yl), x_left.at[1, yl, :, lane(comp)], gs_sem.at[1], gr_sem.at[1], zdev(1))
        send(panel(comp, yl), u.at[yl, 1, 0, :, lane(comp)], gs_sem.at[2], gr_sem.at[2], zdev(-1))

    def send_or_keep(src, dst, s_sem, r_sem, dest):
        mine = is_me(dest)
        @pl.when(jnp.logical_not(mine))
        def _():
            send(src, dst, s_sem, r_sem, dest)
        @pl.when(mine)
        def _():
            pltpu.make_async_copy(src, dst, r_sem).start()

    def finish_send(src, s_sem, dest):
        @pl.when(jnp.logical_not(is_me(dest)))
        def _():
            wait_bytes(src, s_sem)

    slot = (x % 2) * 2 + yl
    l_src[...] = jnp.zeros_like(l_src)
    log_copy.wait()
    for f in range(NX):
        l_src[f, :, 0:RUN] = log_v[0, f : f + 1, :]
    for f in range(NX):
        send_or_keep(l_src.at[f], l_in.at[slot], ls_sem.at[f], lr_sem.at[0], up[f])

    wait_bytes(u.at[other, 0, 0], gr_sem.at[0])
    send(u.at[other, 0, 0], x_left.at[1, other], gs_sem.at[3], gr_sem.at[3], zdev(1))
    send(u.at[other, 0, 0], u.at[other, 1, 0], gs_sem.at[4], gr_sem.at[4], zdev(-1))

    wait_bytes(l_in, lr_sem.at[0])
    for d in range(1, NZ):
        send(l_in, l_z.at[z], ls2_sem.at[0], lr_sem.at[1], zdev(d))
    l_z[z] = l_in[...]

    def build_turned(lo, j):
        u[lo, j, 1, :, 0:NP] = -u[lo, j, 0, :, NP : 2 * NP]
        u[lo, j, 1, :, NP : 2 * NP] = u[lo, j, 0, :, 0:NP]

    def build_weighted(g, psd2):
        for lo in range(2):
            x_psd[g, lo] = (x_left[g, lo].astype(F32) * psd2).astype(BF16)

    def correlate(g):
        count = 2 if g < 2 else 1
        left = x_psd[g].reshape(2 * ST, 2 * NP)
        for lo in range(2):
            right = u[lo, FIRST_J[g] : FIRST_J[g] + count].reshape(count * 2 * ST, 2 * NP)
            product = lax.dot_general(left, right, (((1,), (1,)), ((), ())), preferred_element_type=F32)
            if count == 1:
                product = jnp.concatenate([product, jnp.zeros_like(product)], axis=1)
            c_part[lo, g] = product.reshape(2, 2, 16, 128).astype(BF16)

    def pass_on(half, at):
        wait_bytes(x_left.at[1, half], gr_sem.at[at])
        send(x_left.at[1, half], x_left.at[2, half], gs_sem.at[at + 4], gr_sem.at[at + 4], zdev(1))
        wait_bytes(u.at[half, 1, 0], gr_sem.at[at + 1])
        send(u.at[half, 1, 0], u.at[half, 2, 0], gs_sem.at[at + 5], gr_sem.at[at + 5], zdev(-1))

    obs_copy.wait()
    w_copy.wait()
    for zl in range(2):
        w = w_v[:, zl * ST : (zl + 1) * ST].astype(F32)
        for f in range(NX):
            real = w * obs_v[f, 0, :, zl * ST : (zl + 1) * ST]
            imag = w * obs_v[f, 1, :, zl * ST : (zl + 1) * ST]
            msg[f, zl] = jnp.concatenate([real, imag, w, w], axis=1)

    wait_bytes(u.at[yl, 0, 0], in_sem.at[2])
    for lo in range(2):
        x_left[0, lo] = u[lo, 0, 0]
        build_turned(lo, 0)
    pass_on(yl, 1)

    wait_bytes(l_z.at[pl.ds(0, NZ - 1)], lr_sem.at[1])
    for zz in range(NZ):
        for k in range(4):
            l_rows[k * NZ + zz : k * NZ + zz + 1, :] = l_z[zz, k]
    point = lax.broadcasted_iota(jnp.int32, (128, NP), 1)
    run_of = lax.shift_right_logical(point * 2731, 16)
    spread = (point - run_of * RUN == lax.broadcasted_iota(jnp.int32, (128, NP), 0)).astype(F32)
    spread_rows = jnp.dot(l_rows[...], spread, precision=HIGHEST, preferred_element_type=F32)
    run_row = lax.shift_right_logical(lax.broadcasted_iota(jnp.int32, (32, NP), 1) * 2731, 16)
    log_field = jnp.sum(
        jnp.where(run_row == lax.broadcasted_iota(jnp.int32, (32, NP), 0), spread_rows, 0.0), axis=0, keepdims=True
    )
    psd = jnp.exp(log_field)
    psd2 = jnp.concatenate([psd, psd], axis=1)
    build_weighted(0, psd2)

    pass_on(other, 3)
    for k, (plane, zl, delta, dest) in enumerate(pair_dests):
        send_or_keep(msg.at[plane, zl], e_in.at[delta], es_sem.at[k], er_sem.at[0], dest)
    for lo in range(2):
        build_turned(lo, 1)
    build_weighted(1, psd2)
    correlate(0)

    for half, at in ((yl, 5), (other, 7)):
        wait_bytes(x_left.at[2, half], gr_sem.at[at])
        wait_bytes(u.at[half, 2, 0], gr_sem.at[at + 1])
    for lo in range(2):
        build_turned(lo, 2)
    build_weighted(2, psd2)
    correlate(1)
    correlate(2)

    def pair_terms():
        wait_bytes(e_in, er_sem.at[0])
        lane_at = lax.broadcasted_iota(jnp.int32, (ST, 128), 1)
        same = (lane_at % ST == lax.broadcasted_iota(jnp.int32, (ST, 128), 0)).astype(F32)
        part_at = lane_at // ST

        def turned(block):
            full = lax.dot_general(block, same, (((0,), (0,)), ((), ())), precision=HIGHEST, preferred_element_type=F32)
            result = jnp.where(part_at == 0, full[0:ST], full[ST : 2 * ST])
            result = jnp.where(part_at == 2, full[2 * ST : 3 * ST], result)
            return jnp.where(part_at == 3, full[3 * ST : 4 * ST], result)

        def conj(block):
            return jnp.where(part_at == 1, -block, block)

        slots = (
            (conj(e_in[0]), turned(e_in[1]) + conj(e_in[7])),
            (turned(e_in[2]) + conj(e_in[6]), turned(e_in[3]) + conj(e_in[5])),
            (conj(e_in[4]), jnp.zeros((ST, 128), F32)),
        )
        low = lane_at < 2 * ST
        for g, (first, second) in enumerate(slots):
            d_all[g] = jnp.where(low, first, pltpu.roll(second, 64, 1))
            w_all[g] = jnp.where(low, pltpu.roll(first, 64, 1), second) * QUAD

    def exchange_rest(it, psd):
        phase = lambda k: (ph_s.at[it, k], ph_r.at[it, k])
        s_sem, r_sem = phase(0)
        for d in range(1, NO):
            o, dest = odev(d)
            send(c_part.at[(o // 2) % 2, :, o // 4, o % 2], rs.at[it, d - 1], s_sem, r_sem, dest)
        total = c_part[yl, :, yh, core].astype(F32)
        if it == 0:
            pair_terms()
        wait_bytes(rs.at[it], r_sem)
        for d in range(NO - 1):
            total = total + rs[it, d].astype(F32)
        own_rows = pl.ds(pl.multiple_of(core * 16, 16), 16)
        b_out[it] = (w_all[:, own_rows, :] * total - d_all[:, own_rows, :]).astype(BF16)
        s_sem, r_sem = phase(1)
        for d in range(1, NO):
            send(b_out.at[it], b_full.at[it, yl, :, yh, core], s_sem, r_sem, odev(d)[1])
        b_full[it, yl, :, yh, core] = b_out[it]
        wait_bytes(rs.at[it], r_sem)

        width = 384
        terms = []
        for c in range(2 * NP // width):
            lanes = slice(c * width, (c + 1) * width)
            term = jnp.zeros((1, width), F32)
            for g in range(3):
                count = 2 if g < 2 else 1
                field = jnp.zeros((2 * ST, width), F32)
                for lo in range(2):
                    b = b_full[it, lo, g].reshape(2 * ST, 128)[:, 0 : count * 2 * ST]
                    right = u[lo, FIRST_J[g] : FIRST_J[g] + count, :, :, lanes].reshape(count * 2 * ST, width)
                    field = field + jnp.dot(b, right, preferred_element_type=F32)
                left = x_left[g, :, :, lanes].reshape(2 * ST, width).astype(F32)
                term = term + jnp.sum(left * field, axis=0, keepdims=True)
            terms.append(term)
        half = len(terms) // 2
        mine = jnp.concatenate([terms[k] + terms[half + k] for k in range(half)], axis=1)
        g_mine[it] = mine
        s_sem, r_sem = phase(2)
        for d in range(1, NZ):
            send(g_mine.at[it], g_all.at[it, z], s_sem, r_sem, zdev(d))
        g_all[it, z] = mine
        wait_bytes(g_all.at[it, pl.ds(0, NZ - 1)], r_sem)
        summed = g_all[it, 0]
        for k in range(1, NZ):
            summed = summed + g_all[it, k]
        return QUAD * psd * summed

    def start_mean(it, gradient):
        squares = jnp.broadcast_to(jnp.sum(gradient * gradient, axis=1, keepdims=True), (1, 128))
        s_mine[it] = squares
        for d in range(1, NS):
            send(s_mine.at[it], s_all.at[it, x * NO + me], ph_s.at[it, 3], ph_r.at[it, 3], sdev(d))
        s_all[it, x * NO + me] = squares

    def finish_mean(it):
        wait_bytes(s_all.at[it, pl.ds(0, NS - 1)], ph_r.at[it, 3])
        total = jnp.sum(s_all[it], axis=0)
        return jnp.sqrt(total / ENTRIES + EPSILON)[:, 0:1]

    gradient = exchange_rest(0, psd)
    start_mean(0, gradient)
    wait_bytes(rs.at[0], ph_s.at[0, 0])
    log_field = log_field - DESCENT * gradient / finish_mean(0)

    psd = jnp.exp(log_field)
    psd2 = jnp.concatenate([psd, psd], axis=1)
    for g in range(3):
        build_weighted(g, psd2)
        correlate(g)
    m_mine[...] = log_field
    for k in range(4):
        send_or_keep(m_mine, m_in.at[x], ms_sem.at[k], mr_sem.at[0], down[k])
    gradient = exchange_rest(1, psd)
    start_mean(1, gradient)
    o_mine[...] = gradient
    for k in range(4):
        send_or_keep(o_mine, o_in.at[x], os_sem.at[k], or_sem.at[0], down[k])

    start = (slot * NZ + z) * RUN
    pick = (
        lax.broadcasted_iota(jnp.int32, (NP, 128), 0) == lax.broadcasted_iota(jnp.int32, (NP, 128), 1) + start
    ).astype(F32)

    def run_of_points(rows, parts):
        rows[...] = jnp.zeros_like(rows)
        for f in range(NX):
            rows[f : f + 1, :] = parts[f]
        return jnp.dot(rows[...], pick, precision=HIGHEST, preferred_element_type=F32)[0:NX, 0:RUN]

    wait_bytes(m_in, mr_sem.at[0])
    own_field = run_of_points(rows_m, m_in)
    wait_bytes(o_in, or_sem.at[0])
    own_gradient = run_of_points(rows_o, o_in)
    out[0] = own_field - DESCENT * own_gradient / finish_mean(1)

    for k in range(9):
        wait_bytes(x_left.at[1, 0], gs_sem.at[k])
    for f in range(NX):
        finish_send(l_src.at[f], ls_sem.at[f], up[f])
    wait_bytes(l_z.at[pl.ds(0, NZ - 1)], ls2_sem.at[0])
    for k, (plane, zl, delta, dest) in enumerate(pair_dests):
        finish_send(msg.at[plane, zl], es_sem.at[k], dest)
    for it in range(ITERS):
        if it > 0:
            wait_bytes(rs.at[it], ph_s.at[it, 0])
        wait_bytes(rs.at[it], ph_s.at[it, 1])
        wait_bytes(g_all.at[it, pl.ds(0, NZ - 1)], ph_s.at[it, 2])
        wait_bytes(s_all.at[it, pl.ds(0, NS - 1)], ph_s.at[it, 3])
    for k in range(4):
        finish_send(m_mine, ms_sem.at[k], down[k])
        finish_send(o_mine, os_sem.at[k], down[k])


def body(green_panel, log_psd, observed, pair_weights):
    vmem = pltpu.VMEM
    dma = pltpu.SemaphoreType.DMA
    return pl.pallas_call(
        kernel,
        out_shape=jax.ShapeDtypeStruct(log_psd.shape, F32),
        in_specs=[
            pl.BlockSpec(memory_space=pltpu.HBM),
            pl.BlockSpec(memory_space=pltpu.HBM),
            pl.BlockSpec(memory_space=pltpu.HBM),
            pl.BlockSpec(memory_space=pltpu.HBM),
        ],
        out_specs=pl.BlockSpec(memory_space=pltpu.VMEM),
        scratch_shapes=[
            vmem((2, 3, 2, ST, 2 * NP), BF16),
            vmem((3, 2, ST, 2 * NP), BF16),
            vmem((3, 2, ST, 2 * NP), BF16),
            vmem((1, NX, RUN), F32),
            vmem((NX, 2, ST, 2 * ST), F32),
            vmem((ST, 2 * ST), jnp.int32),
            vmem((NX, 2, ST, 128), F32),
            vmem((NZ, ST, 128), F32),
            vmem((3, ST, 128), F32),
            vmem((3, ST, 128), F32),
            vmem((NX, 1, 128), F32),
            vmem((4, 1, 128), F32),
            vmem((NZ, 4, 1, 128), F32),
            vmem((32, 128), F32),
            vmem((2, 3, 2, 2, 16, 128), BF16),
            vmem((ITERS, NO - 1, 3, 16, 128), BF16),
            vmem((ITERS, 3, 16, 128), BF16),
            vmem((ITERS, 2, 3, 2, 2, 16, 128), BF16),
            vmem((ITERS, 1, NP), F32),
            vmem((ITERS, NZ, 1, NP), F32),
            vmem((ITERS, 1, 128), F32),
            vmem((ITERS, NS, 1, 128), F32),
            vmem((1, NP), F32),
            vmem((1, NP), F32),
            vmem((NX, 1, NP), F32),
            vmem((NX, 1, NP), F32),
            vmem((8, NP), F32),
            vmem((8, NP), F32),
            dma((4,)),
            dma((9,)),
            dma((9,)),
            dma((1,)),
            dma((8,)),
            dma((2,)),
            dma((4,)),
            dma((1,)),
            dma((ITERS, 4)),
            dma((ITERS, 4)),
            dma((1,)),
            dma((4,)),
            dma((1,)),
            dma((4,)),
        ],
        compiler_params=pltpu.CompilerParams(
            collective_id=0, has_side_effects=True, vmem_limit_bytes=63 * 1024 * 1024
        ),
    )(green_panel, log_psd, jnp.swapaxes(observed, 2, 3), pair_weights.T)


def solution(mesh):
    return jax.shard_map(
        body,
        mesh=mesh,
        in_specs=(
            P(None, None, "col", "pts"),
            P("pts", None, ("row", "col")),
            P(None, None, "row", "col"),
            P("row", "col"),
        ),
        out_specs=P("pts", None, ("row", "col")),
        check_vma=False,
    )
```

```python
import functools

import jax
import jax.numpy as jnp
from jax import lax
from jax.experimental import pallas as pl
from jax.experimental.pallas import tpu as pltpu
from jax.sharding import PartitionSpec as P

MESH = pl.DeviceIdType.MESH
HIGHEST = lax.Precision.HIGHEST
F32 = jnp.float32
BF16 = jnp.bfloat16

ITERS = 2
NX = 4
NZ = 8
NO = 8
NS = NX * NO
ST = 32
NP = 768
RUN = 24
ENTRIES = 4 * 6144
QUAD = 1.0 / 6144
EPSILON = 1e-06
DESCENT = 0.1

FIRST_J = (0, 1, 2)


def wait_bytes(ref, sem):
    pltpu.make_async_copy(ref, ref, sem).wait()


def kernel(
    green, logp, obs, weights, out,
    u, x_left, x_psd, log_v, obs_v, w_v, msg, e_in, d_all, w_all,
    l_src, l_in, l_z, l_rows, c_part, rs, b_out, b_full, g_mine, g_all, s_mine, s_all,
    m_mine, o_mine, m_in, o_in, rows_m, rows_o,
    in_sem, gr_sem, gs_sem, er_sem, es_sem, lr_sem, ls_sem, ls2_sem,
    ph_r, ph_s, mr_sem, ms_sem, or_sem, os_sem,
):
    row = lax.axis_index("row")
    col = lax.axis_index("col")
    core = lax.axis_index("pts")
    yh, x = row // 4, row % 4
    yl, z = col // 8, col % 8
    mine_at = x * NO + yh * 4 + yl * 2 + core
    other = 1 - yl

    def dev(x_, yh_, yl_, z_, core_):
        return (yh_ * 4 + x_, yl_ * 8 + z_, core_)

    z_steps = (4, 3, 5, 2, 6, 1, 7)
    y_at = yh * 2 + yl
    o_steps = [(dy, dc) for dy in (2, 1, 3, 0) for dc in (1, 0) if dy or dc]
    s_steps = [(dx, dy, dc) for dx in (2, 1, 3, 0) for dy in (2, 1, 3, 0) for dc in (1, 0) if dx or dy or dc]
    s_steps.sort(key=lambda step: -min(step[0], 4 - step[0]) - min(step[1], 4 - step[1]) - 0.5 * step[2])

    def zdev(d):
        return dev(x, yh, yl, (z + d) % NZ, core)

    def odev(dy, dc):
        to_y, to_core = (y_at + dy) % 4, (core + dc) % 2
        return to_y, to_core, dev(x, to_y // 2, to_y % 2, z, to_core)

    def sdev(dx, dy, dc):
        to_y = (y_at + dy) % 4
        return dev((x + dx) % NX, to_y // 2, to_y % 2, z, (core + dc) % 2)

    def is_me(dest):
        return jnp.logical_and(jnp.logical_and(dest[0] == row, dest[1] == col), dest[2] == core)

    obs_copy = pltpu.make_async_copy(obs, obs_v, in_sem.at[0])
    w_copy = pltpu.make_async_copy(weights, w_v, in_sem.at[1])
    log_copy = pltpu.make_async_copy(logp, log_v, in_sem.at[3])
    log_copy.start()
    obs_copy.start()
    w_copy.start()

    def panel(comp, lo):
        start = pl.multiple_of((yh * 2 + lo) * NP, 128)
        return green.at[x, comp, :, pl.ds(start, NP)]

    for comp in range(2):
        pltpu.make_async_copy(panel(comp, yl), u.at[yl, 0, 0, :, pl.ds(comp * NP, NP)], in_sem.at[2]).start()

    def centre(zi, zj):
        delta = (zj - zi) % NZ
        from_i = jnp.where(delta >= 2, 1, 0)
        from_j = jnp.where(delta == 7, 0, jnp.where(delta == 4, 2, 1))
        zc = jnp.where(delta <= 3, zi + from_i, zj + from_j) % NZ
        return delta, zc

    def pair_dest(plane, zl):
        delta, zc = centre(2 * x + zl, z)
        swap = jnp.logical_or(delta == 0, delta >= 4)
        return delta, dev(plane, jnp.where(swap, yl, yh), jnp.where(swap, yh, yl), zc, core)

    pair_dests = []
    for plane in range(NX):
        for zl in range(2):
            pair_dests.append((plane, zl) + pair_dest(plane, zl))
    offsets = ((0, 0), (0, 1), (-1, 1), (-1, 2), (2, -2), (2, -1), (1, -1), (1, 0))
    pair_sources = []
    for delta in range(NZ):
        zi, zj = (z + offsets[delta][0]) % NZ, (z + offsets[delta][1]) % NZ
        if 1 <= delta <= 3:
            pair_sources.append(dev(zi // 2, yh, yl, zj, core))
        else:
            pair_sources.append(dev(zi // 2, yl, yh, zj, core))

    up = [dev(plane, yh, x // 2, z, core) for plane in range(NX)]
    down = [dev(2 * yl + k // 2, yh, k % 2, z, core) for k in range(4)]

    log_copy.wait()
    l_src[...] = jnp.zeros_like(l_src)
    for f in range(NX):
        l_src[f, :, 0:RUN] = log_v[0, f : f + 1, :]

    partner = dev(x, yh, other, z, core)
    diagonal = {d: dev(x, yh, other, (z + d) % NZ, core) for d in (1, -1)}
    barrier = pltpu.get_barrier_semaphore()
    expected = jnp.int32(NZ - 1 + NO - 1 + 2 + 8)
    for dest in (partner, zdev(1), zdev(-1), diagonal[1], diagonal[-1]):
        pl.semaphore_signal(barrier, inc=1, device_id=dest, device_id_type=MESH)
    for d in z_steps[:-2]:
        pl.semaphore_signal(barrier, inc=1, device_id=zdev(d), device_id_type=MESH)
    for step in o_steps:
        pl.semaphore_signal(barrier, inc=1, device_id=odev(*step)[2], device_id_type=MESH)
    expected = expected + 1
    for dest in up + down:
        @pl.when(jnp.logical_not(is_me(dest)))
        def _(dest=dest):
            pl.semaphore_signal(barrier, inc=1, device_id=dest, device_id_type=MESH)
        expected = expected - is_me(dest).astype(jnp.int32)
    for delta, source in enumerate(pair_sources):
        if not 1 <= delta <= 3:
            @pl.when(jnp.logical_not(is_me(source)))
            def _(source=source):
                pl.semaphore_signal(barrier, inc=1, device_id=source, device_id_type=MESH)
    for plane, zl, delta, dest in pair_dests:
        swap = jnp.logical_or(delta == 0, delta >= 4)
        expected = expected + jnp.logical_and(swap, jnp.logical_not(is_me(dest))).astype(jnp.int32)
    pl.semaphore_wait(barrier, expected)

    def send(src, dst, s_sem, r_sem, dest):
        copy = pltpu.make_async_remote_copy(
            src_ref=src, dst_ref=dst, send_sem=s_sem, recv_sem=r_sem, device_id=dest, device_id_type=MESH
        )
        copy.start()
        return copy

    lanes_of = [pl.ds(comp * NP, NP) for comp in range(2)]

    def send_or_keep(src, dst, s_sem, r_sem, dest):
        mine = is_me(dest)
        @pl.when(jnp.logical_not(mine))
        def _():
            send(src, dst, s_sem, r_sem, dest)
        @pl.when(mine)
        def _():
            pltpu.make_async_copy(src, dst, r_sem).start()

    def finish_send(src, s_sem, dest):
        @pl.when(jnp.logical_not(is_me(dest)))
        def _():
            wait_bytes(src, s_sem)

    slot = (x % 2) * 2 + yl
    for f in range(NX):
        send_or_keep(l_src.at[f], l_in.at[slot], ls_sem.at[f], lr_sem.at[0], up[f])

    def launch(k, comp, src, dst, dest):
        send(src, dst.at[:, lanes_of[comp]], gs_sem.at[comp, k], gr_sem.at[comp, k], dest)

    for comp in range(2):
        launch(1, comp, panel(comp, yl), x_left.at[1, yl], zdev(1))
        launch(2, comp, panel(comp, yl), u.at[yl, 1, 0], zdev(-1))
        launch(0, comp, panel(comp, other), u.at[yl, 0, 0], partner)
    for comp in range(2):
        launch(3, comp, panel(comp, other), x_left.at[1, yl], diagonal[1])
        launch(4, comp, panel(comp, other), u.at[yl, 1, 0], diagonal[-1])

    def build_turned(lo, j):
        u[lo, j, 1, :, 0:NP] = -u[lo, j, 0, :, NP : 2 * NP]
        u[lo, j, 1, :, NP : 2 * NP] = u[lo, j, 0, :, 0:NP]

    def build_weighted(g, psd2):
        for lo in range(2):
            x_psd[g, lo] = (x_left[g, lo].astype(F32) * psd2).astype(BF16)

    def correlate(g):
        count = 2 if g < 2 else 1
        left = x_psd[g].reshape(2 * ST, 2 * NP)
        for lo in range(2):
            right = u[lo, FIRST_J[g] : FIRST_J[g] + count].reshape(count * 2 * ST, 2 * NP)
            product = lax.dot_general(left, right, (((1,), (1,)), ((), ())), preferred_element_type=F32)
            if count == 1:
                product = jnp.concatenate([product, jnp.zeros_like(product)], axis=1)
            c_part[lo, g] = product.reshape(2, 2, 16, 128).astype(BF16)

    def arrive(k, comp, dst):
        wait_bytes(dst.at[:, lanes_of[comp]], gr_sem.at[comp, k])

    def pass_on(half, at):
        for comp in range(2):
            piece = x_left.at[1, half]
            arrive(at, comp, piece)
            launch(at + 4, comp, piece.at[:, lanes_of[comp]], x_left.at[2, half], zdev(1))
            piece = u.at[half, 1, 0]
            arrive(at + 1, comp, piece)
            launch(at + 5, comp, piece.at[:, lanes_of[comp]], u.at[half, 2, 0], zdev(-1))

    obs_copy.wait()
    w_copy.wait()
    for zl in range(2):
        w = w_v[:, zl * ST : (zl + 1) * ST].astype(F32)
        for f in range(NX):
            real = w * obs_v[f, 0, :, zl * ST : (zl + 1) * ST]
            imag = w * obs_v[f, 1, :, zl * ST : (zl + 1) * ST]
            msg[f, zl] = jnp.concatenate([real, imag, w, w], axis=1)

    wait_bytes(l_in, lr_sem.at[0])
    for d in z_steps:
        send(l_in, l_z.at[z], ls2_sem.at[0], lr_sem.at[1], zdev(d))
    l_z[z] = l_in[...]
    pass_on(yl, 1)
    wait_bytes(u.at[yl, 0, 0], in_sem.at[2])
    pass_on(other, 3)
    wait_bytes(l_z.at[pl.ds(0, NZ - 1)], lr_sem.at[1])
    for k, (plane, zl, delta, dest) in enumerate(pair_dests):
        send_or_keep(msg.at[plane, zl], e_in.at[delta], es_sem.at[k], er_sem.at[0], dest)
    for comp in range(2):
        arrive(0, comp, u.at[other, 0, 0])
    for lo in range(2):
        x_left[0, lo] = u[lo, 0, 0]
        build_turned(lo, 0)
        build_turned(lo, 1)

    for zz in range(NZ):
        for k in range(4):
            l_rows[k * NZ + zz : k * NZ + zz + 1, :] = l_z[zz, k]
    point = lax.broadcasted_iota(jnp.int32, (128, NP), 1)
    run_of = lax.shift_right_logical(point * 2731, 16)
    spread = (point - run_of * RUN == lax.broadcasted_iota(jnp.int32, (128, NP), 0)).astype(F32)
    spread_rows = jnp.dot(l_rows[...], spread, precision=HIGHEST, preferred_element_type=F32)
    run_row = lax.shift_right_logical(lax.broadcasted_iota(jnp.int32, (32, NP), 1) * 2731, 16)
    log_field = jnp.sum(
        jnp.where(run_row == lax.broadcasted_iota(jnp.int32, (32, NP), 0), spread_rows, 0.0), axis=0, keepdims=True
    )
    psd = jnp.exp(log_field)
    psd2 = jnp.concatenate([psd, psd], axis=1)
    build_weighted(0, psd2)

    build_weighted(1, psd2)
    correlate(0)

    for half, at in ((yl, 5), (other, 7)):
        for comp in range(2):
            arrive(at, comp, x_left.at[2, half])
            arrive(at + 1, comp, u.at[half, 2, 0])
    for lo in range(2):
        build_turned(lo, 2)
    build_weighted(2, psd2)
    correlate(1)
    correlate(2)

    def pair_terms():
        wait_bytes(e_in, er_sem.at[0])
        lane_at = lax.broadcasted_iota(jnp.int32, (ST, 128), 1)
        same = (lane_at % ST == lax.broadcasted_iota(jnp.int32, (ST, 128), 0)).astype(F32)
        part_at = lane_at // ST

        def turned(block):
            full = lax.dot_general(block, same, (((0,), (0,)), ((), ())), precision=HIGHEST, preferred_element_type=F32)
            result = jnp.where(part_at == 0, full[0:ST], full[ST : 2 * ST])
            result = jnp.where(part_at == 2, full[2 * ST : 3 * ST], result)
            return jnp.where(part_at == 3, full[3 * ST : 4 * ST], result)

        def conj(block):
            return jnp.where(part_at == 1, -block, block)

        slots = (
            (conj(e_in[0]), turned(e_in[1]) + conj(e_in[7])),
            (turned(e_in[2]) + conj(e_in[6]), turned(e_in[3]) + conj(e_in[5])),
            (conj(e_in[4]), jnp.zeros((ST, 128), F32)),
        )
        low = lane_at < 2 * ST
        for g, (first, second) in enumerate(slots):
            d_all[g] = jnp.where(low, first, pltpu.roll(second, 64, 1))
            w_all[g] = jnp.where(low, pltpu.roll(first, 64, 1), second) * QUAD

    def finish_phase(it, phase):
        sizes = (rs.at[it], rs.at[it], g_all.at[it, pl.ds(0, NZ - 1)], s_all.at[it, pl.ds(0, NS - 1)])
        wait_bytes(sizes[phase], ph_s.at[it, phase])

    def finish_start():
        for comp in range(2):
            for k in range(9):
                wait_bytes(x_left.at[1, 0, :, lanes_of[comp]], gs_sem.at[comp, k])
        for f in range(NX):
            finish_send(l_src.at[f], ls_sem.at[f], up[f])
        wait_bytes(l_z.at[pl.ds(0, NZ - 1)], ls2_sem.at[0])
        for k, (plane, zl, delta, dest) in enumerate(pair_dests):
            finish_send(msg.at[plane, zl], es_sem.at[k], dest)
        for phase in range(1, 4):
            finish_phase(0, phase)

    def exchange_rest(it, psd):
        phase = lambda k: (ph_s.at[it, k], ph_r.at[it, k])
        s_sem, r_sem = phase(0)
        for k, step in enumerate(o_steps):
            to_y, to_core, dest = odev(*step)
            send(c_part.at[to_y % 2, :, to_y // 2, to_core], rs.at[it, k], s_sem, r_sem, dest)
        total = c_part[yl, :, yh, core].astype(F32)
        if it == 0:
            pair_terms()
        else:
            finish_start()
        wait_bytes(rs.at[it], r_sem)
        for d in range(NO - 1):
            total = total + rs[it, d].astype(F32)
        own_rows = pl.ds(pl.multiple_of(core * 16, 16), 16)
        b_out[it] = (w_all[:, own_rows, :] * total - d_all[:, own_rows, :]).astype(BF16)
        s_sem, r_sem = phase(1)
        for step in o_steps:
            send(b_out.at[it], b_full.at[it, yl, :, yh, core], s_sem, r_sem, odev(*step)[2])
        b_full[it, yl, :, yh, core] = b_out[it]
        finish_phase(it, 0)
        wait_bytes(rs.at[it], r_sem)

        width = 384
        terms = []
        for c in range(2 * NP // width):
            lanes = slice(c * width, (c + 1) * width)
            term = jnp.zeros((1, width), F32)
            for g in range(3):
                count = 2 if g < 2 else 1
                field = jnp.zeros((2 * ST, width), F32)
                for lo in range(2):
                    b = b_full[it, lo, g].reshape(2 * ST, 128)[:, 0 : count * 2 * ST]
                    right = u[lo, FIRST_J[g] : FIRST_J[g] + count, :, :, lanes].reshape(count * 2 * ST, width)
                    field = field + jnp.dot(b, right, preferred_element_type=F32)
                left = x_left[g, :, :, lanes].reshape(2 * ST, width).astype(F32)
                term = term + jnp.sum(left * field, axis=0, keepdims=True)
            terms.append(term)
        half = len(terms) // 2
        mine = jnp.concatenate([terms[k] + terms[half + k] for k in range(half)], axis=1)
        g_mine[it] = mine
        s_sem, r_sem = phase(2)
        for d in z_steps:
            send(g_mine.at[it], g_all.at[it, z], s_sem, r_sem, zdev(d))
        g_all[it, z] = mine
        wait_bytes(g_all.at[it, pl.ds(0, NZ - 1)], r_sem)
        summed = g_all[it, 0]
        for k in range(1, NZ):
            summed = summed + g_all[it, k]
        return QUAD * psd * summed

    def start_mean(it, gradient):
        squares = jnp.broadcast_to(jnp.sum(gradient * gradient, axis=1, keepdims=True), (1, 128))
        s_mine[it] = squares
        for step in s_steps:
            send(s_mine.at[it], s_all.at[it, mine_at], ph_s.at[it, 3], ph_r.at[it, 3], sdev(*step))
        s_all[it, mine_at] = squares

    def finish_mean(it):
        wait_bytes(s_all.at[it, pl.ds(0, NS - 1)], ph_r.at[it, 3])
        total = jnp.sum(s_all[it], axis=0)
        return jnp.sqrt(total / ENTRIES + EPSILON)[:, 0:1]

    gradient = exchange_rest(0, psd)
    start_mean(0, gradient)
    log_field = log_field - DESCENT * gradient / finish_mean(0)

    psd = jnp.exp(log_field)
    psd2 = jnp.concatenate([psd, psd], axis=1)
    for g in range(3):
        build_weighted(g, psd2)
        correlate(g)
    m_mine[...] = log_field
    for k in range(4):
        send_or_keep(m_mine, m_in.at[x], ms_sem.at[k], mr_sem.at[0], down[k])
    gradient = exchange_rest(1, psd)
    start_mean(1, gradient)
    o_mine[...] = gradient
    for k in range(4):
        send_or_keep(o_mine, o_in.at[x], os_sem.at[k], or_sem.at[0], down[k])

    start = (slot * NZ + z) * RUN
    pick = (
        lax.broadcasted_iota(jnp.int32, (NP, 128), 0) == lax.broadcasted_iota(jnp.int32, (NP, 128), 1) + start
    ).astype(F32)

    def run_of_points(rows, parts):
        rows[...] = jnp.zeros_like(rows)
        for f in range(NX):
            rows[f : f + 1, :] = parts[f]
        return jnp.dot(rows[...], pick, precision=HIGHEST, preferred_element_type=F32)[0:NX, 0:RUN]

    wait_bytes(m_in, mr_sem.at[0])
    own_field = run_of_points(rows_m, m_in)
    wait_bytes(o_in, or_sem.at[0])
    own_gradient = run_of_points(rows_o, o_in)
    out[0] = own_field - DESCENT * own_gradient / finish_mean(1)

    finish_phase(1, 1)
    finish_phase(1, 2)
    finish_phase(1, 3)
    for k in range(4):
        finish_send(m_mine, ms_sem.at[k], down[k])
        finish_send(o_mine, os_sem.at[k], down[k])


def body(green_panel, log_psd, observed, pair_weights):
    vmem = pltpu.VMEM
    dma = pltpu.SemaphoreType.DMA
    return pl.pallas_call(
        kernel,
        out_shape=jax.ShapeDtypeStruct(log_psd.shape, F32),
        in_specs=[
            pl.BlockSpec(memory_space=pltpu.HBM),
            pl.BlockSpec(memory_space=pltpu.HBM),
            pl.BlockSpec(memory_space=pltpu.HBM),
            pl.BlockSpec(memory_space=pltpu.HBM),
        ],
        out_specs=pl.BlockSpec(memory_space=pltpu.VMEM),
        scratch_shapes=[
            vmem((2, 3, 2, ST, 2 * NP), BF16),
            vmem((3, 2, ST, 2 * NP), BF16),
            vmem((3, 2, ST, 2 * NP), BF16),
            vmem((1, NX, RUN), F32),
            vmem((NX, 2, ST, 2 * ST), F32),
            vmem((ST, 2 * ST), jnp.int32),
            vmem((NX, 2, ST, 128), F32),
            vmem((NZ, ST, 128), F32),
            vmem((3, ST, 128), F32),
            vmem((3, ST, 128), F32),
            vmem((NX, 1, 128), F32),
            vmem((4, 1, 128), F32),
            vmem((NZ, 4, 1, 128), F32),
            vmem((32, 128), F32),
            vmem((2, 3, 2, 2, 16, 128), BF16),
            vmem((ITERS, NO - 1, 3, 16, 128), BF16),
            vmem((ITERS, 3, 16, 128), BF16),
            vmem((ITERS, 2, 3, 2, 2, 16, 128), BF16),
            vmem((ITERS, 1, NP), F32),
            vmem((ITERS, NZ, 1, NP), F32),
            vmem((ITERS, 1, 128), F32),
            vmem((ITERS, NS, 1, 128), F32),
            vmem((1, NP), F32),
            vmem((1, NP), F32),
            vmem((NX, 1, NP), F32),
            vmem((NX, 1, NP), F32),
            vmem((8, NP), F32),
            vmem((8, NP), F32),
            dma((4,)),
            dma((2, 9)),
            dma((2, 9)),
            dma((1,)),
            dma((8,)),
            dma((2,)),
            dma((4,)),
            dma((1,)),
            dma((ITERS, 4)),
            dma((ITERS, 4)),
            dma((1,)),
            dma((4,)),
            dma((1,)),
            dma((4,)),
        ],
        compiler_params=pltpu.CompilerParams(
            collective_id=0, has_side_effects=True, vmem_limit_bytes=63 * 1024 * 1024
        ),
    )(green_panel, log_psd, jnp.swapaxes(observed, 2, 3), pair_weights.T)


def solution(mesh):
    return jax.shard_map(
        body,
        mesh=mesh,
        in_specs=(
            P(None, None, "col", "pts"),
            P("pts", None, ("row", "col")),
            P(None, None, "row", "col"),
            P("row", "col"),
        ),
        out_specs=P("pts", None, ("row", "col")),
        check_vma=False,
    )
```

```python
import functools

import jax
import jax.numpy as jnp
from jax import lax
from jax.experimental import pallas as pl
from jax.experimental.pallas import tpu as pltpu
from jax.sharding import PartitionSpec as P

MESH = pl.DeviceIdType.MESH
HIGHEST = lax.Precision.HIGHEST
F32 = jnp.float32
BF16 = jnp.bfloat16

ITERS = 2
NX = 4
NZ = 8
NO = 8
NS = NX * NO
ST = 32
NP = 768
RUN = 24
ENTRIES = 4 * 6144
QUAD = 1.0 / 6144
EPSILON = 1e-06
DESCENT = 0.1

FIRST_J = (0, 1, 2)


def wait_bytes(ref, sem):
    pltpu.make_async_copy(ref, ref, sem).wait()


def kernel(
    green, logp, obs, weights, out,
    u, x_left, x_psd, away, log_v, obs_v, w_v, msg, e_in, d_all, w_all,
    l_src, l_in, l_z, l_rows, c_part, rs, b_out, b_full, g_mine, g_all, s_mine, s_all,
    m_mine, o_mine, m_in, o_in, rows_m, rows_o,
    in_sem, gr_sem, gs_sem, er_sem, es_sem, lr_sem, ls_sem, ls2_sem,
    tokens, ph_r, ph_s, mr_sem, ms_sem, or_sem, os_sem,
):
    row = lax.axis_index("row")
    col = lax.axis_index("col")
    core = lax.axis_index("pts")
    yh, x = row // 4, row % 4
    yl, z = col // 8, col % 8
    mine_at = x * NO + yh * 4 + yl * 2 + core
    other = 1 - yl

    def dev(x_, yh_, yl_, z_, core_):
        return (yh_ * 4 + x_, yl_ * 8 + z_, core_)

    z_steps = (4, 3, 5, 2, 6, 1, 7)
    y_at = yh * 2 + yl
    o_steps = [(dy, dc) for dy in (2, 1, 3, 0) for dc in (1, 0) if dy or dc]
    s_steps = [(dx, dy, dc) for dx in (2, 1, 3, 0) for dy in (2, 1, 3, 0) for dc in (1, 0) if dx or dy or dc]
    s_steps.sort(key=lambda step: -min(step[0], 4 - step[0]) - min(step[1], 4 - step[1]) - 0.5 * step[2])

    def zdev(d):
        return dev(x, yh, yl, (z + d) % NZ, core)

    def odev(dy, dc):
        to_y, to_core = (y_at + dy) % 4, (core + dc) % 2
        return to_y, to_core, dev(x, to_y // 2, to_y % 2, z, to_core)

    def sdev(dx, dy, dc):
        to_y = (y_at + dy) % 4
        return dev((x + dx) % NX, to_y // 2, to_y % 2, z, (core + dc) % 2)

    def is_me(dest):
        return jnp.logical_and(jnp.logical_and(dest[0] == row, dest[1] == col), dest[2] == core)

    obs_copy = pltpu.make_async_copy(obs, obs_v, in_sem.at[0])
    w_copy = pltpu.make_async_copy(weights, w_v, in_sem.at[1])
    log_copy = pltpu.make_async_copy(logp, log_v, in_sem.at[3])
    log_copy.start()
    obs_copy.start()
    w_copy.start()

    def panel(comp, lo):
        start = pl.multiple_of((yh * 2 + lo) * NP, 128)
        return green.at[x, comp, :, pl.ds(start, NP)]

    lanes_of = [pl.ds(comp * NP, NP) for comp in range(2)]
    staged = []
    for comp in range(2):
        staged.append(pltpu.make_async_copy(panel(comp, yl), u.at[yl, 0, 0, :, lanes_of[comp]], in_sem.at[4 + comp]))
        staged.append(pltpu.make_async_copy(panel(comp, other), away.at[:, lanes_of[comp]], in_sem.at[6 + comp]))
    for copy in staged:
        copy.start()

    def centre(zi, zj):
        delta = (zj - zi) % NZ
        from_i = jnp.where(delta >= 2, 1, 0)
        from_j = jnp.where(delta == 7, 0, jnp.where(delta == 4, 2, 1))
        zc = jnp.where(delta <= 3, zi + from_i, zj + from_j) % NZ
        return delta, zc

    def pair_dest(plane, zl):
        delta, zc = centre(2 * x + zl, z)
        swap = jnp.logical_or(delta == 0, delta >= 4)
        return delta, dev(plane, jnp.where(swap, yl, yh), jnp.where(swap, yh, yl), zc, core)

    pair_dests = []
    for plane in range(NX):
        for zl in range(2):
            pair_dests.append((plane, zl) + pair_dest(plane, zl))
    up = [dev(plane, yh, x // 2, z, core) for plane in range(NX)]
    down = [dev(2 * yl + k // 2, yh, k % 2, z, core) for k in range(4)]

    log_copy.wait()
    l_src[...] = jnp.zeros_like(l_src)
    for f in range(NX):
        l_src[f, :, 0:RUN] = log_v[0, f : f + 1, :]

    partner = dev(x, yh, other, z, core)
    diagonal = {d: dev(x, yh, other, (z + d) % NZ, core) for d in (1, -1)}
    y_near = [odev(dy, 0)[2] for dy in (1, 3)]
    across = dev(x, 1 - yh, other, z, core)
    sibling = dev(x, yh, yl, z, 1 - core)
    z_near = [zdev(d) for d in (1, -1, 2, -2)]
    xy_near = [dev((x + dx) % NX, yh, lo, z, core) for dx in (2, 1, 3) for lo in (other, yl)]
    near = xy_near + [diagonal[1], diagonal[-1], partner, across, sibling] + z_near
    barrier = pltpu.get_barrier_semaphore()
    for dest in near:
        pl.semaphore_signal(barrier, inc=1, device_id=dest, device_id_type=MESH)
    for copy in staged:
        copy.wait()
    pl.semaphore_wait(barrier, len(near))

    def pass_token(k, dests):
        for dest in dests:
            pl.semaphore_signal(tokens.at[k], inc=1, device_id=dest, device_id_type=MESH)


    def send(src, dst, s_sem, r_sem, dest):
        copy = pltpu.make_async_remote_copy(
            src_ref=src, dst_ref=dst, send_sem=s_sem, recv_sem=r_sem, device_id=dest, device_id_type=MESH
        )
        copy.start()
        return copy

    def send_or_keep(src, dst, s_sem, r_sem, dest):
        mine = is_me(dest)
        @pl.when(jnp.logical_not(mine))
        def _():
            send(src, dst, s_sem, r_sem, dest)
        @pl.when(mine)
        def _():
            pltpu.make_async_copy(src, dst, r_sem).start()

    def finish_send(src, s_sem, dest):
        @pl.when(jnp.logical_not(is_me(dest)))
        def _():
            wait_bytes(src, s_sem)

    slot = (x % 2) * 2 + yl
    for f in range(NX):
        send_or_keep(l_src.at[f], l_in.at[slot], ls_sem.at[f], lr_sem.at[0], up[f])

    def launch(k, comp, src, dst, dest):
        send(src, dst.at[:, lanes_of[comp]], gs_sem.at[comp, k], gr_sem.at[comp, k], dest)

    own = u.at[yl, 0, 0]
    for comp in range(2):
        launch(1, comp, own.at[:, lanes_of[comp]], x_left.at[1, yl], zdev(1))
        launch(2, comp, own.at[:, lanes_of[comp]], u.at[yl, 1, 0], zdev(-1))
        launch(0, comp, away.at[:, lanes_of[comp]], u.at[yl, 0, 0], partner)
    for comp in range(2):
        launch(3, comp, away.at[:, lanes_of[comp]], x_left.at[1, yl], diagonal[1])
        launch(4, comp, away.at[:, lanes_of[comp]], u.at[yl, 1, 0], diagonal[-1])

    def build_turned(lo, j):
        u[lo, j, 1, :, 0:NP] = -u[lo, j, 0, :, NP : 2 * NP]
        u[lo, j, 1, :, NP : 2 * NP] = u[lo, j, 0, :, 0:NP]

    def build_weighted(g, psd2):
        for lo in range(2):
            x_psd[g, lo] = (x_left[g, lo].astype(F32) * psd2).astype(BF16)

    def correlate(g, halves):
        count = 2 if g < 2 else 1
        left = x_psd[g].reshape(2 * ST, 2 * NP)
        for lo in halves:
            right = u[lo, FIRST_J[g] : FIRST_J[g] + count].reshape(count * 2 * ST, 2 * NP)
            product = lax.dot_general(left, right, (((1,), (1,)), ((), ())), preferred_element_type=F32)
            if count == 1:
                product = jnp.concatenate([product, jnp.zeros_like(product)], axis=1)
            c_part[lo, g] = product.reshape(2, 2, 16, 128).astype(BF16)

    def arrive(k, comp, dst):
        wait_bytes(dst.at[:, lanes_of[comp]], gr_sem.at[comp, k])

    def pass_on(half, at):
        for comp in range(2):
            piece = x_left.at[1, half]
            arrive(at, comp, piece)
            launch(at + 4, comp, piece.at[:, lanes_of[comp]], x_left.at[2, half], zdev(1))
            piece = u.at[half, 1, 0]
            arrive(at + 1, comp, piece)
            launch(at + 5, comp, piece.at[:, lanes_of[comp]], u.at[half, 2, 0], zdev(-1))

    pass_token(0, z_near)

    obs_copy.wait()
    w_copy.wait()
    for zl in range(2):
        w = w_v[:, zl * ST : (zl + 1) * ST].astype(F32)
        for f in range(NX):
            real = w * obs_v[f, 0, :, zl * ST : (zl + 1) * ST]
            imag = w * obs_v[f, 1, :, zl * ST : (zl + 1) * ST]
            msg[f, zl] = jnp.concatenate([real, imag, w, w], axis=1).astype(BF16)

    pl.semaphore_wait(tokens.at[0], len(z_near))
    pass_token(1, y_near)
    wait_bytes(l_in, lr_sem.at[0])
    for d in z_steps:
        send(l_in, l_z.at[z], ls2_sem.at[0], lr_sem.at[1], zdev(d))
    l_z[z] = l_in[...]
    pass_on(yl, 1)
    pass_on(other, 3)
    pl.semaphore_wait(tokens.at[1], len(y_near))
    for comp in range(2):
        arrive(0, comp, u.at[other, 0, 0])
    pass_token(2, [sibling])
    for k, (plane, zl, delta, dest) in enumerate(pair_dests):
        send_or_keep(msg.at[plane, zl], e_in.at[delta], es_sem.at[k], er_sem.at[0], dest)
    for lo in range(2):
        x_left[0, lo] = u[lo, 0, 0]
        build_turned(lo, 0)
        build_turned(lo, 1)

    wait_bytes(l_z.at[pl.ds(0, NZ - 1)], lr_sem.at[1])
    for zz in range(NZ):
        for k in range(4):
            l_rows[k * NZ + zz : k * NZ + zz + 1, :] = l_z[zz, k]
    point = lax.broadcasted_iota(jnp.int32, (128, NP), 1)
    run_of = lax.shift_right_logical(point * 2731, 16)
    spread = (point - run_of * RUN == lax.broadcasted_iota(jnp.int32, (128, NP), 0)).astype(F32)
    spread_rows = jnp.dot(l_rows[...], spread, precision=HIGHEST, preferred_element_type=F32)
    run_row = lax.shift_right_logical(lax.broadcasted_iota(jnp.int32, (32, NP), 1) * 2731, 16)
    log_field = jnp.sum(
        jnp.where(run_row == lax.broadcasted_iota(jnp.int32, (32, NP), 0), spread_rows, 0.0), axis=0, keepdims=True
    )
    psd = jnp.exp(log_field)
    psd2 = jnp.concatenate([psd, psd], axis=1)
    build_weighted(0, psd2)

    build_weighted(1, psd2)
    correlate(0, (yl, other))

    pl.semaphore_wait(tokens.at[2], 1)

    for half, at in ((yl, 5), (other, 7)):
        for comp in range(2):
            arrive(at, comp, x_left.at[2, half])
            arrive(at + 1, comp, u.at[half, 2, 0])
    for lo in range(2):
        build_turned(lo, 2)
    build_weighted(2, psd2)

    def pair_terms():
        wait_bytes(e_in, er_sem.at[0])
        lane_at = lax.broadcasted_iota(jnp.int32, (ST, 128), 1)
        same = (lane_at % ST == lax.broadcasted_iota(jnp.int32, (ST, 128), 0)).astype(BF16)
        part_at = lane_at // ST

        def turned(block):
            full = lax.dot_general(block, same, (((0,), (0,)), ((), ())), preferred_element_type=F32)
            result = jnp.where(part_at == 0, full[0:ST], full[ST : 2 * ST])
            result = jnp.where(part_at == 2, full[2 * ST : 3 * ST], result)
            return jnp.where(part_at == 3, full[3 * ST : 4 * ST], result)

        def conj(block):
            block = block.astype(F32)
            return jnp.where(part_at == 1, -block, block)

        slots = (
            (conj(e_in[0]), turned(e_in[1]) + conj(e_in[7])),
            (turned(e_in[2]) + conj(e_in[6]), turned(e_in[3]) + conj(e_in[5])),
            (conj(e_in[4]), jnp.zeros((ST, 128), F32)),
        )
        low = lane_at < 2 * ST
        for g, (first, second) in enumerate(slots):
            d_all[g] = jnp.where(low, first, pltpu.roll(second, 64, 1))
            w_all[g] = jnp.where(low, pltpu.roll(first, 64, 1), second) * QUAD

    def finish_phase(it, phase):
        sizes = (rs.at[it], rs.at[it], g_all.at[it, pl.ds(0, NZ - 1)], s_all.at[it, pl.ds(0, NS - 1)])
        wait_bytes(sizes[phase], ph_s.at[it, phase])

    def finish_start():
        for comp in range(2):
            for k in range(9):
                wait_bytes(x_left.at[1, 0, :, lanes_of[comp]], gs_sem.at[comp, k])
        for f in range(NX):
            finish_send(l_src.at[f], ls_sem.at[f], up[f])
        wait_bytes(l_z.at[pl.ds(0, NZ - 1)], ls2_sem.at[0])
        for k, (plane, zl, delta, dest) in enumerate(pair_dests):
            finish_send(msg.at[plane, zl], es_sem.at[k], dest)
        for phase in range(1, 4):
            finish_phase(0, phase)

    def exchange_rest(it, psd):
        phase = lambda k: (ph_s.at[it, k], ph_r.at[it, k])
        s_sem, r_sem = phase(0)
        for half, odd in ((yl, 0), (other, 1)):
            for g in range(1 if it == 0 else 0, 3):
                correlate(g, (half,))
            for k, step in enumerate(o_steps):
                if step[0] % 2 == odd:
                    to_y, to_core, dest = odev(*step)
                    send(c_part.at[half, :, to_y // 2, to_core], rs.at[it, k], s_sem, r_sem, dest)
        total = c_part[yl, :, yh, core].astype(F32)
        if it == 0:
            pair_terms()
        else:
            finish_start()
        wait_bytes(rs.at[it], r_sem)
        for d in range(NO - 1):
            total = total + rs[it, d].astype(F32)
        own_rows = pl.ds(pl.multiple_of(core * 16, 16), 16)
        b_out[it] = (w_all[:, own_rows, :] * total - d_all[:, own_rows, :]).astype(BF16)
        s_sem, r_sem = phase(1)
        for step in o_steps:
            send(b_out.at[it], b_full.at[it, yl, :, yh, core], s_sem, r_sem, odev(*step)[2])
        b_full[it, yl, :, yh, core] = b_out[it]
        finish_phase(it, 0)
        wait_bytes(rs.at[it], r_sem)

        width = 384
        terms = []
        for c in range(2 * NP // width):
            lanes = slice(c * width, (c + 1) * width)
            term = jnp.zeros((1, width), F32)
            for g in range(3):
                count = 2 if g < 2 else 1
                field = jnp.zeros((2 * ST, width), F32)
                for lo in range(2):
                    b = b_full[it, lo, g].reshape(2 * ST, 128)[:, 0 : count * 2 * ST]
                    right = u[lo, FIRST_J[g] : FIRST_J[g] + count, :, :, lanes].reshape(count * 2 * ST, width)
                    field = field + jnp.dot(b, right, preferred_element_type=F32)
                left = x_left[g, :, :, lanes].reshape(2 * ST, width).astype(F32)
                term = term + jnp.sum(left * field, axis=0, keepdims=True)
            terms.append(term)
        half = len(terms) // 2
        mine = jnp.concatenate([terms[k] + terms[half + k] for k in range(half)], axis=1)
        g_mine[it] = mine
        s_sem, r_sem = phase(2)
        for d in z_steps:
            send(g_mine.at[it], g_all.at[it, z], s_sem, r_sem, zdev(d))
        g_all[it, z] = mine
        wait_bytes(g_all.at[it, pl.ds(0, NZ - 1)], r_sem)
        summed = g_all[it, 0]
        for k in range(1, NZ):
            summed = summed + g_all[it, k]
        return QUAD * psd * summed

    def start_mean(it, gradient):
        squares = gradient[:, 0:128] * gradient[:, 0:128]
        for k in range(1, NP // 128):
            squares = squares + gradient[:, k * 128 : (k + 1) * 128] * gradient[:, k * 128 : (k + 1) * 128]
        s_mine[it] = squares
        for step in s_steps:
            send(s_mine.at[it], s_all.at[it, mine_at], ph_s.at[it, 3], ph_r.at[it, 3], sdev(*step))
        s_all[it, mine_at] = squares

    def finish_mean(it):
        wait_bytes(s_all.at[it, pl.ds(0, NS - 1)], ph_r.at[it, 3])
        total = jnp.sum(jnp.sum(s_all[it], axis=0), axis=1, keepdims=True)
        return jnp.sqrt(total / ENTRIES + EPSILON)

    gradient = exchange_rest(0, psd)
    start_mean(0, gradient)
    log_field = log_field - DESCENT * gradient / finish_mean(0)

    psd = jnp.exp(log_field)
    psd2 = jnp.concatenate([psd, psd], axis=1)
    for g in range(3):
        build_weighted(g, psd2)
    m_mine[...] = log_field
    for k in range(4):
        send_or_keep(m_mine, m_in.at[x], ms_sem.at[k], mr_sem.at[0], down[k])
    gradient = exchange_rest(1, psd)
    start_mean(1, gradient)
    o_mine[...] = gradient
    for k in range(4):
        send_or_keep(o_mine, o_in.at[x], os_sem.at[k], or_sem.at[0], down[k])

    start = (slot * NZ + z) * RUN
    pick = (
        lax.broadcasted_iota(jnp.int32, (NP, 128), 0) == lax.broadcasted_iota(jnp.int32, (NP, 128), 1) + start
    ).astype(F32)

    def run_of_points(rows, parts):
        rows[...] = jnp.zeros_like(rows)
        for f in range(NX):
            rows[f : f + 1, :] = parts[f]
        return jnp.dot(rows[...], pick, precision=HIGHEST, preferred_element_type=F32)[0:NX, 0:RUN]

    wait_bytes(m_in, mr_sem.at[0])
    own_field = run_of_points(rows_m, m_in)
    wait_bytes(o_in, or_sem.at[0])
    own_gradient = run_of_points(rows_o, o_in)
    out[0] = own_field - DESCENT * own_gradient / finish_mean(1)

    finish_phase(1, 1)
    finish_phase(1, 2)
    finish_phase(1, 3)
    for k in range(4):
        finish_send(m_mine, ms_sem.at[k], down[k])
        finish_send(o_mine, os_sem.at[k], down[k])


def body(green_panel, log_psd, observed, pair_weights):
    vmem = pltpu.VMEM
    dma = pltpu.SemaphoreType.DMA
    return pl.pallas_call(
        kernel,
        out_shape=jax.ShapeDtypeStruct(log_psd.shape, F32),
        in_specs=[
            pl.BlockSpec(memory_space=pltpu.HBM),
            pl.BlockSpec(memory_space=pltpu.HBM),
            pl.BlockSpec(memory_space=pltpu.HBM),
            pl.BlockSpec(memory_space=pltpu.HBM),
        ],
        out_specs=pl.BlockSpec(memory_space=pltpu.VMEM),
        scratch_shapes=[
            vmem((2, 3, 2, ST, 2 * NP), BF16),
            vmem((3, 2, ST, 2 * NP), BF16),
            vmem((3, 2, ST, 2 * NP), BF16),
            vmem((ST, 2 * NP), BF16),
            vmem((1, NX, RUN), F32),
            vmem((NX, 2, ST, 2 * ST), F32),
            vmem((ST, 2 * ST), jnp.int32),
            vmem((NX, 2, ST, 128), BF16),
            vmem((NZ, ST, 128), BF16),
            vmem((3, ST, 128), F32),
            vmem((3, ST, 128), F32),
            vmem((NX, 1, 128), F32),
            vmem((4, 1, 128), F32),
            vmem((NZ, 4, 1, 128), F32),
            vmem((32, 128), F32),
            vmem((2, 3, 2, 2, 16, 128), BF16),
            vmem((ITERS, NO - 1, 3, 16, 128), BF16),
            vmem((ITERS, 3, 16, 128), BF16),
            vmem((ITERS, 2, 3, 2, 2, 16, 128), BF16),
            vmem((ITERS, 1, NP), F32),
            vmem((ITERS, NZ, 1, NP), F32),
            vmem((ITERS, 1, 128), F32),
            vmem((ITERS, NS, 1, 128), F32),
            vmem((1, NP), F32),
            vmem((1, NP), F32),
            vmem((NX, 1, NP), F32),
            vmem((NX, 1, NP), F32),
            vmem((8, NP), F32),
            vmem((8, NP), F32),
            dma((8,)),
            dma((2, 9)),
            dma((2, 9)),
            dma((1,)),
            dma((8,)),
            dma((2,)),
            dma((4,)),
            dma((1,)),
            pltpu.SemaphoreType.REGULAR((3,)),
            dma((ITERS, 4)),
            dma((ITERS, 4)),
            dma((1,)),
            dma((4,)),
            dma((1,)),
            dma((4,)),
        ],
        compiler_params=pltpu.CompilerParams(
            collective_id=0, has_side_effects=True, vmem_limit_bytes=63 * 1024 * 1024
        ),
    )(green_panel, log_psd, jnp.swapaxes(observed, 2, 3), pair_weights.T)


def solution(mesh):
    return jax.shard_map(
        body,
        mesh=mesh,
        in_specs=(
            P(None, None, "col", "pts"),
            P("pts", None, ("row", "col")),
            P(None, None, "row", "col"),
            P("row", "col"),
        ),
        out_specs=P("pts", None, ("row", "col")),
        check_vma=False,
    )
```

```python
import functools

import jax
import jax.numpy as jnp
from jax import lax
from jax.experimental import pallas as pl
from jax.experimental.pallas import tpu as pltpu
from jax.sharding import PartitionSpec as P

MESH = pl.DeviceIdType.MESH
HIGHEST = lax.Precision.HIGHEST
F32 = jnp.float32
BF16 = jnp.bfloat16

ITERS = 2
NX = 4
NZ = 8
NO = 8
NS = NX * NO
ST = 32
NP = 768
RUN = 24
ENTRIES = 4 * 6144
QUAD = 1.0 / 6144
EPSILON = 1e-06
DESCENT = 0.1

PAIRS = ((0, 0), (0, 1), (1, 1), (1, 2), (2, 2))


def wait_bytes(ref, sem):
    pltpu.make_async_copy(ref, ref, sem).wait()


def kernel(
    green, logp, obs, weights, out,
    u, x_left, x_psd, away, log_v, obs_v, w_v, msg, e_in, d_all, w_all,
    l_src, l_in, l_z, l_rows, pair_rows, pair_all, c_part, core_in, y_all, b_full, g_mine, g_all, s_mine, s_all,
    m_mine, o_mine, m_in, o_in, rows_m, rows_o,
    in_sem, gr_sem, gs_sem, er_sem, es_sem, lr_sem, ls_sem, ls2_sem,
    tokens, pt_sem, ph_r, ph_s, mr_sem, ms_sem, or_sem, os_sem,
):
    row = lax.axis_index("row")
    col = lax.axis_index("col")
    core = lax.axis_index("pts")
    yh, x = row // 4, row % 4
    yl, z = col // 8, col % 8
    mine_at = x * NO + yh * 4 + yl * 2 + core
    other = 1 - yl

    def dev(x_, yh_, yl_, z_, core_):
        return (yh_ * 4 + x_, yl_ * 8 + z_, core_)

    z_steps = (4, 3, 5, 2, 6, 1, 7)
    y_at = yh * 2 + yl
    o_steps = [(dy, dc) for dy in (2, 1, 3, 0) for dc in (1, 0) if dy or dc]
    s_steps = [(dx, dy, dc) for dx in (2, 1, 3, 0) for dy in (2, 1, 3, 0) for dc in (1, 0) if dx or dy or dc]
    s_steps.sort(key=lambda step: -min(step[0], 4 - step[0]) - min(step[1], 4 - step[1]) - 0.5 * step[2])

    def zdev(d):
        return dev(x, yh, yl, (z + d) % NZ, core)

    def odev(dy, dc):
        to_y, to_core = (y_at + dy) % 4, (core + dc) % 2
        return to_y, to_core, dev(x, to_y // 2, to_y % 2, z, to_core)

    def sdev(dx, dy, dc):
        to_y = (y_at + dy) % 4
        return dev((x + dx) % NX, to_y // 2, to_y % 2, z, (core + dc) % 2)

    def is_me(dest):
        return jnp.logical_and(jnp.logical_and(dest[0] == row, dest[1] == col), dest[2] == core)

    obs_copy = pltpu.make_async_copy(obs, obs_v, in_sem.at[0])
    w_copy = pltpu.make_async_copy(weights, w_v, in_sem.at[1])
    log_copy = pltpu.make_async_copy(logp, log_v, in_sem.at[3])
    log_copy.start()
    obs_copy.start()
    w_copy.start()

    def panel(comp, lo):
        start = pl.multiple_of((yh * 2 + lo) * NP, 128)
        return green.at[x, comp, :, pl.ds(start, NP)]

    lanes_of = [pl.ds(comp * NP, NP) for comp in range(2)]
    staged = []
    for comp in range(2):
        staged.append(pltpu.make_async_copy(panel(comp, yl), u.at[0, yl, 0, :, lanes_of[comp]], in_sem.at[4 + comp]))
        staged.append(pltpu.make_async_copy(panel(comp, other), away.at[:, lanes_of[comp]], in_sem.at[6 + comp]))
    for copy in staged:
        copy.start()

    def centre(zi, zj):
        delta = (zj - zi) % NZ
        from_i = jnp.where(delta >= 2, 1, 0)
        from_j = jnp.where(delta == 7, 0, jnp.where(delta == 4, 2, 1))
        zc = jnp.where(delta <= 3, zi + from_i, zj + from_j) % NZ
        return delta, zc

    def pair_dest(plane, zl):
        delta, zc = centre(2 * x + zl, z)
        swap = jnp.logical_or(delta == 0, delta >= 4)
        return delta, dev(plane, jnp.where(swap, yl, yh), jnp.where(swap, yh, yl), zc, core)

    pair_dests = []
    for plane in range(NX):
        for zl in range(2):
            pair_dests.append((plane, zl) + pair_dest(plane, zl))
    up = [dev(plane, yh, x // 2, z, core) for plane in range(NX)]
    down = [dev(2 * yl + k // 2, yh, k % 2, z, core) for k in range(4)]

    log_copy.wait()
    l_src[...] = jnp.zeros_like(l_src)
    for f in range(NX):
        l_src[f, :, 0:RUN] = log_v[0, f : f + 1, :]

    partner = dev(x, yh, other, z, core)
    diagonal = {d: dev(x, yh, other, (z + d) % NZ, core) for d in (1, -1)}
    y_near = [odev(dy, 0)[2] for dy in (1, 3)]
    across = dev(x, 1 - yh, other, z, core)
    sibling = dev(x, yh, yl, z, 1 - core)
    z_near = [zdev(d) for d in (1, -1, 2, -2)]
    xy_near = [dev((x + dx) % NX, yh, lo, z, core) for dx in (2, 1, 3) for lo in (other, yl)]
    near = xy_near + [diagonal[1], diagonal[-1], partner, across, sibling] + z_near
    barrier = pltpu.get_barrier_semaphore()
    for dest in near:
        pl.semaphore_signal(barrier, inc=1, device_id=dest, device_id_type=MESH)
    for copy in staged:
        copy.wait()
    pl.semaphore_wait(barrier, len(near))

    def pass_token(k, dests):
        for dest in dests:
            pl.semaphore_signal(tokens.at[k], inc=1, device_id=dest, device_id_type=MESH)


    def send(src, dst, s_sem, r_sem, dest):
        copy = pltpu.make_async_remote_copy(
            src_ref=src, dst_ref=dst, send_sem=s_sem, recv_sem=r_sem, device_id=dest, device_id_type=MESH
        )
        copy.start()
        return copy

    def send_or_keep(src, dst, s_sem, r_sem, dest):
        mine = is_me(dest)
        @pl.when(jnp.logical_not(mine))
        def _():
            send(src, dst, s_sem, r_sem, dest)
        @pl.when(mine)
        def _():
            pltpu.make_async_copy(src, dst, r_sem).start()

    def finish_send(src, s_sem, dest):
        @pl.when(jnp.logical_not(is_me(dest)))
        def _():
            wait_bytes(src, s_sem)

    slot = (x % 2) * 2 + yl
    for f in range(NX):
        send_or_keep(l_src.at[f], l_in.at[slot], ls_sem.at[f], lr_sem.at[0], up[f])

    def launch(k, comp, src, dst, dest):
        send(src, dst.at[:, lanes_of[comp]], gs_sem.at[comp, k], gr_sem.at[comp, k], dest)

    own = u.at[0, yl, 0]
    for comp in range(2):
        launch(1, comp, own.at[:, lanes_of[comp]], x_left.at[1, yl], zdev(1))
        launch(2, comp, own.at[:, lanes_of[comp]], u.at[1, yl, 0], zdev(-1))
        launch(0, comp, away.at[:, lanes_of[comp]], u.at[0, yl, 0], partner)
    for comp in range(2):
        launch(3, comp, away.at[:, lanes_of[comp]], x_left.at[1, yl], diagonal[1])
        launch(4, comp, away.at[:, lanes_of[comp]], u.at[1, yl, 0], diagonal[-1])

    def build_turned(lo, j):
        u[j, lo, 1, :, 0:NP] = -u[j, lo, 0, :, NP : 2 * NP]
        u[j, lo, 1, :, NP : 2 * NP] = u[j, lo, 0, :, 0:NP]

    def build_weighted(g, psd2):
        for lo in range(2):
            x_psd[g, lo] = (x_left[g, lo].astype(F32) * psd2).astype(BF16)

    def correlate(it, j):
        tiles = [k for k, pair in enumerate(PAIRS) if pair[1] == j]
        first = PAIRS[tiles[0]][0]
        left = x_psd[first : first + len(tiles)].reshape(len(tiles) * 2 * ST, 2 * NP)
        right = u[j].reshape(4 * ST, 2 * NP)
        product = lax.dot_general(left, right, (((1,), (1,)), ((), ())), preferred_element_type=F32)
        for k, tile in enumerate(tiles):
            block = product[k * 2 * ST : (k + 1) * 2 * ST].reshape(2, 2, 16, 128).astype(BF16)
            for half in range(2):
                c_part[it, half, tile] = block[:, half]

    def arrive(k, comp, dst):
        wait_bytes(dst.at[:, lanes_of[comp]], gr_sem.at[comp, k])

    def pass_on(half, at):
        for comp in range(2):
            piece = x_left.at[1, half]
            arrive(at, comp, piece)
            launch(at + 4, comp, piece.at[:, lanes_of[comp]], x_left.at[2, half], zdev(1))
            piece = u.at[1, half, 0]
            arrive(at + 1, comp, piece)
            launch(at + 5, comp, piece.at[:, lanes_of[comp]], u.at[2, half, 0], zdev(-1))

    pass_token(0, z_near)

    obs_copy.wait()
    w_copy.wait()
    for zl in range(2):
        w = w_v[:, zl * ST : (zl + 1) * ST].astype(F32)
        for f in range(NX):
            real = w * obs_v[f, 0, :, zl * ST : (zl + 1) * ST]
            imag = w * obs_v[f, 1, :, zl * ST : (zl + 1) * ST]
            msg[f, zl] = jnp.concatenate([real, imag, w, w], axis=1).astype(BF16)

    pl.semaphore_wait(tokens.at[0], len(z_near))
    pass_token(1, y_near)
    wait_bytes(l_in, lr_sem.at[0])
    for d in z_steps:
        send(l_in, l_z.at[z], ls2_sem.at[0], lr_sem.at[1], zdev(d))
    l_z[z] = l_in[...]
    pass_on(yl, 1)
    pass_on(other, 3)
    pl.semaphore_wait(tokens.at[1], len(y_near))
    for comp in range(2):
        arrive(0, comp, u.at[0, other, 0])
    for k, (plane, zl, delta, dest) in enumerate(pair_dests):
        send_or_keep(msg.at[plane, zl], e_in.at[delta], es_sem.at[k], er_sem.at[0], dest)
    for lo in range(2):
        x_left[0, lo] = u[0, lo, 0]
        build_turned(lo, 0)
        build_turned(lo, 1)

    wait_bytes(l_z.at[pl.ds(0, NZ - 1)], lr_sem.at[1])
    for zz in range(NZ):
        for k in range(4):
            l_rows[k * NZ + zz : k * NZ + zz + 1, :] = l_z[zz, k]
    point = lax.broadcasted_iota(jnp.int32, (128, NP), 1)
    run_of = lax.shift_right_logical(point * 2731, 16)
    spread = (point - run_of * RUN == lax.broadcasted_iota(jnp.int32, (128, NP), 0)).astype(F32)
    spread_rows = jnp.dot(l_rows[...], spread, precision=HIGHEST, preferred_element_type=F32)
    run_row = lax.shift_right_logical(lax.broadcasted_iota(jnp.int32, (32, NP), 1) * 2731, 16)
    log_field = jnp.sum(
        jnp.where(run_row == lax.broadcasted_iota(jnp.int32, (32, NP), 0), spread_rows, 0.0), axis=0, keepdims=True
    )
    psd = jnp.exp(log_field)
    psd2 = jnp.concatenate([psd, psd], axis=1)
    build_weighted(0, psd2)

    build_weighted(1, psd2)
    correlate(0, 0)
    correlate(0, 1)

    for half, at in ((yl, 5), (other, 7)):
        for comp in range(2):
            arrive(at, comp, x_left.at[2, half])
            arrive(at + 1, comp, u.at[2, half, 0])
    for lo in range(2):
        build_turned(lo, 2)
    build_weighted(2, psd2)
    correlate(0, 2)

    def pair_terms():
        wait_bytes(e_in, er_sem.at[0])
        lane_at = lax.broadcasted_iota(jnp.int32, (ST, 128), 1)
        same = (lane_at % ST == lax.broadcasted_iota(jnp.int32, (ST, 128), 0)).astype(BF16)
        part_at = lane_at // ST

        def turned(block):
            full = lax.dot_general(block, same, (((0,), (0,)), ((), ())), preferred_element_type=F32)
            result = jnp.where(part_at == 0, full[0:ST], full[ST : 2 * ST])
            result = jnp.where(part_at == 2, full[2 * ST : 3 * ST], result)
            return jnp.where(part_at == 3, full[3 * ST : 4 * ST], result)

        def conj(block):
            block = block.astype(F32)
            return jnp.where(part_at == 1, -block, block)

        blocks = (
            conj(e_in[0]),
            turned(e_in[1]) + conj(e_in[7]),
            turned(e_in[2]) + conj(e_in[6]),
            turned(e_in[3]) + conj(e_in[5]),
            conj(e_in[4]),
        )
        for tile, block in enumerate(blocks):
            pair_rows[tile] = jnp.where(yl == 0, block, pltpu.roll(block, 64, 1))
        own_rows = pl.ds(pl.multiple_of(core * 16, 16), 16)
        pair_all[y_at] = pair_rows[:, own_rows, :].astype(BF16)
        for dy in (2, 1, 3):
            send(pair_all.at[y_at], pair_all.at[y_at], pt_sem.at[0], pt_sem.at[1], odev(dy, 0)[2])

    def pair_tiles():
        wait_bytes(pair_all.at[pl.ds(0, 3)], pt_sem.at[1])
        low = lax.broadcasted_iota(jnp.int32, (16, 128), 1) < 64
        for tile in range(len(PAIRS)):
            for hi in range(2):
                first = pair_all[2 * hi, tile].astype(F32)
                second = pair_all[2 * hi + 1, tile].astype(F32)
                d_all[tile, hi] = jnp.where(low, first, second)
                w_all[tile, hi] = jnp.where(low, pltpu.roll(first, 64, 1), pltpu.roll(second, 64, 1)) * QUAD

    def finish_phase(it, phase):
        sizes = (
            core_in.at[it], y_all.at[it, pl.ds(0, 3)], g_all.at[it, pl.ds(0, NZ - 1)],
            s_all.at[it, pl.ds(0, NS - 1)], core_in.at[it],
        )
        wait_bytes(sizes[phase], ph_s.at[it, phase])

    def finish_start():
        for comp in range(2):
            for k in range(9):
                wait_bytes(x_left.at[1, 0, :, lanes_of[comp]], gs_sem.at[comp, k])
        for f in range(NX):
            finish_send(l_src.at[f], ls_sem.at[f], up[f])
        wait_bytes(l_z.at[pl.ds(0, NZ - 1)], ls2_sem.at[0])
        for k, (plane, zl, delta, dest) in enumerate(pair_dests):
            finish_send(msg.at[plane, zl], es_sem.at[k], dest)
        wait_bytes(pair_all.at[pl.ds(0, 3)], pt_sem.at[0])
        for phase in range(5):
            finish_phase(0, phase)

    def exchange_rest(it, psd):
        phase = lambda k: (ph_s.at[it, k], ph_r.at[it, k])
        s_sem, r_sem = phase(0)
        send(c_part.at[it, 1 - core], core_in.at[it], s_sem, r_sem, sibling)
        wait_bytes(core_in.at[it], r_sem)
        y_all[it, y_at] = (c_part[it, core].astype(F32) + core_in[it].astype(F32)).astype(BF16)
        s_sem, r_sem = phase(1)
        for dy in (2, 1, 3):
            send(y_all.at[it, y_at], y_all.at[it, y_at], s_sem, r_sem, odev(dy, 0)[2])
        if it == 0:
            pair_terms()
            pair_tiles()
        else:
            finish_start()
        wait_bytes(y_all.at[it, pl.ds(0, 3)], r_sem)
        total = y_all[it, 0].astype(F32)
        for k in range(1, 4):
            total = total + y_all[it, k].astype(F32)
        b_full[it, core] = (w_all[...] * total - d_all[...]).astype(BF16)
        s_sem, r_sem = phase(4)
        send(b_full.at[it, core], b_full.at[it, core], s_sem, r_sem, sibling)
        wait_bytes(core_in.at[it], r_sem)

        width = 384
        terms = []
        for c in range(2 * NP // width):
            lanes = slice(c * width, (c + 1) * width)
            term = jnp.zeros((1, width), F32)
            for g in range(3):
                tiles = [k for k, pair in enumerate(PAIRS) if pair[0] == g]
                first = PAIRS[tiles[0]][1]
                b = jnp.concatenate(
                    [
                        jnp.concatenate([b_full[it, half, tile, hi] for hi in range(2) for half in range(2)], axis=0)
                        for tile in tiles
                    ],
                    axis=1,
                )
                right = u[first : first + len(tiles), :, :, :, lanes].reshape(len(tiles) * 4 * ST, width)
                field = jnp.dot(b, right, preferred_element_type=F32)
                left = x_left[g, :, :, lanes].reshape(2 * ST, width).astype(F32)
                term = term + jnp.sum(left * field, axis=0, keepdims=True)
            terms.append(term)
        half = len(terms) // 2
        mine = jnp.concatenate([terms[k] + terms[half + k] for k in range(half)], axis=1)
        g_mine[it] = mine
        s_sem, r_sem = phase(2)
        for d in z_steps:
            send(g_mine.at[it], g_all.at[it, z], s_sem, r_sem, zdev(d))
        g_all[it, z] = mine
        wait_bytes(g_all.at[it, pl.ds(0, NZ - 1)], r_sem)
        summed = g_all[it, 0]
        for k in range(1, NZ):
            summed = summed + g_all[it, k]
        return QUAD * psd * summed

    def start_mean(it, gradient):
        squares = gradient[:, 0:128] * gradient[:, 0:128]
        for k in range(1, NP // 128):
            squares = squares + gradient[:, k * 128 : (k + 1) * 128] * gradient[:, k * 128 : (k + 1) * 128]
        s_mine[it] = squares
        for step in s_steps:
            send(s_mine.at[it], s_all.at[it, mine_at], ph_s.at[it, 3], ph_r.at[it, 3], sdev(*step))
        s_all[it, mine_at] = squares

    def finish_mean(it):
        wait_bytes(s_all.at[it, pl.ds(0, NS - 1)], ph_r.at[it, 3])
        total = jnp.sum(jnp.sum(s_all[it], axis=0), axis=1, keepdims=True)
        return jnp.sqrt(total / ENTRIES + EPSILON)

    gradient = exchange_rest(0, psd)
    start_mean(0, gradient)
    log_field = log_field - DESCENT * gradient / finish_mean(0)

    psd = jnp.exp(log_field)
    psd2 = jnp.concatenate([psd, psd], axis=1)
    for g in range(3):
        build_weighted(g, psd2)
    for j in range(3):
        correlate(1, j)
    m_mine[...] = log_field
    for k in range(4):
        send_or_keep(m_mine, m_in.at[x], ms_sem.at[k], mr_sem.at[0], down[k])
    gradient = exchange_rest(1, psd)
    start_mean(1, gradient)
    o_mine[...] = gradient
    for k in range(4):
        send_or_keep(o_mine, o_in.at[x], os_sem.at[k], or_sem.at[0], down[k])

    start = (slot * NZ + z) * RUN
    pick = (
        lax.broadcasted_iota(jnp.int32, (NP, 128), 0) == lax.broadcasted_iota(jnp.int32, (NP, 128), 1) + start
    ).astype(F32)

    def run_of_points(rows, parts):
        rows[...] = jnp.zeros_like(rows)
        for f in range(NX):
            rows[f : f + 1, :] = parts[f]
        return jnp.dot(rows[...], pick, precision=HIGHEST, preferred_element_type=F32)[0:NX, 0:RUN]

    wait_bytes(m_in, mr_sem.at[0])
    own_field = run_of_points(rows_m, m_in)
    wait_bytes(o_in, or_sem.at[0])
    own_gradient = run_of_points(rows_o, o_in)
    out[0] = own_field - DESCENT * own_gradient / finish_mean(1)

    for phase in range(5):
        finish_phase(1, phase)
    for k in range(4):
        finish_send(m_mine, ms_sem.at[k], down[k])
        finish_send(o_mine, os_sem.at[k], down[k])


def body(green_panel, log_psd, observed, pair_weights):
    vmem = pltpu.VMEM
    dma = pltpu.SemaphoreType.DMA
    return pl.pallas_call(
        kernel,
        out_shape=jax.ShapeDtypeStruct(log_psd.shape, F32),
        in_specs=[
            pl.BlockSpec(memory_space=pltpu.HBM),
            pl.BlockSpec(memory_space=pltpu.HBM),
            pl.BlockSpec(memory_space=pltpu.HBM),
            pl.BlockSpec(memory_space=pltpu.HBM),
        ],
        out_specs=pl.BlockSpec(memory_space=pltpu.VMEM),
        scratch_shapes=[
            vmem((3, 2, 2, ST, 2 * NP), BF16),
            vmem((3, 2, ST, 2 * NP), BF16),
            vmem((3, 2, ST, 2 * NP), BF16),
            vmem((ST, 2 * NP), BF16),
            vmem((1, NX, RUN), F32),
            vmem((NX, 2, ST, 2 * ST), F32),
            vmem((ST, 2 * ST), jnp.int32),
            vmem((NX, 2, ST, 128), BF16),
            vmem((NZ, ST, 128), BF16),
            vmem((5, 2, 16, 128), F32),
            vmem((5, 2, 16, 128), F32),
            vmem((NX, 1, 128), F32),
            vmem((4, 1, 128), F32),
            vmem((NZ, 4, 1, 128), F32),
            vmem((32, 128), F32),
            vmem((5, ST, 128), F32),
            vmem((4, 5, 16, 128), BF16),
            vmem((ITERS, 2, 5, 2, 16, 128), BF16),
            vmem((ITERS, 5, 2, 16, 128), BF16),
            vmem((ITERS, 4, 5, 2, 16, 128), BF16),
            vmem((ITERS, 2, 5, 2, 16, 128), BF16),
            vmem((ITERS, 1, NP), F32),
            vmem((ITERS, NZ, 1, NP), F32),
            vmem((ITERS, 1, 128), F32),
            vmem((ITERS, NS, 1, 128), F32),
            vmem((1, NP), F32),
            vmem((1, NP), F32),
            vmem((NX, 1, NP), F32),
            vmem((NX, 1, NP), F32),
            vmem((8, NP), F32),
            vmem((8, NP), F32),
            dma((8,)),
            dma((2, 9)),
            dma((2, 9)),
            dma((1,)),
            dma((8,)),
            dma((2,)),
            dma((4,)),
            dma((1,)),
            pltpu.SemaphoreType.REGULAR((2,)),
            dma((2,)),
            dma((ITERS, 5)),
            dma((ITERS, 5)),
            dma((1,)),
            dma((4,)),
            dma((1,)),
            dma((4,)),
        ],
        compiler_params=pltpu.CompilerParams(
            collective_id=0, has_side_effects=True, vmem_limit_bytes=63 * 1024 * 1024
        ),
    )(green_panel, log_psd, jnp.swapaxes(observed, 2, 3), pair_weights.T)


def solution(mesh):
    return jax.shard_map(
        body,
        mesh=mesh,
        in_specs=(
            P(None, None, "col", "pts"),
            P("pts", None, ("row", "col")),
            P(None, None, "row", "col"),
            P("row", "col"),
        ),
        out_specs=P("pts", None, ("row", "col")),
        check_vma=False,
    )
```

```python
import functools

import jax
import jax.numpy as jnp
from jax import lax
from jax.experimental import pallas as pl
from jax.experimental.pallas import tpu as pltpu
from jax.sharding import PartitionSpec as P

MESH = pl.DeviceIdType.MESH
HIGHEST = lax.Precision.HIGHEST
F32 = jnp.float32
BF16 = jnp.bfloat16

ITERS = 2
NX = 4
NZ = 8
NO = 8
NS = NX * NO
ST = 32
NP = 768
RUN = 24
ENTRIES = 4 * 6144
QUAD = 1.0 / 6144
EPSILON = 1e-06
DESCENT = 0.1

PAIRS = ((0, 0), (0, 1), (1, 1), (1, 2), (2, 2))


def wait_bytes(ref, sem):
    pltpu.make_async_copy(ref, ref, sem).wait()


def kernel(
    green, logp, obs, weights, out,
    u, x_left, x_psd, away, log_v, obs_v, w_v, msg, e_in, d_all, w_all,
    l_src, l_in, l_z, l_rows, pair_rows, pair_all, c_part, core_in, y_all, b_full, g_mine, g_all, s_mine, s_all,
    m_mine, o_mine, m_in, o_in, rows_m, rows_o,
    in_sem, gr_sem, gs_sem, er_sem, es_sem, lr_sem, ls_sem, ls2_sem,
    tokens, pt_sem, ph_r, ph_s, mr_sem, ms_sem, or_sem, os_sem,
):
    row = lax.axis_index("row")
    col = lax.axis_index("col")
    core = lax.axis_index("pts")
    yh, x = row // 4, row % 4
    yl, z = col // 8, col % 8
    mine_at = x * NO + yh * 4 + yl * 2 + core
    other = 1 - yl

    def dev(x_, yh_, yl_, z_, core_):
        return (yh_ * 4 + x_, yl_ * 8 + z_, core_)

    z_steps = (4, 3, 5, 2, 6, 1, 7)
    y_at = yh * 2 + yl
    o_steps = [(dy, dc) for dy in (2, 1, 3, 0) for dc in (1, 0) if dy or dc]
    s_steps = [(dx, dy, dc) for dx in (2, 1, 3, 0) for dy in (2, 1, 3, 0) for dc in (1, 0) if dx or dy or dc]
    s_steps.sort(key=lambda step: -min(step[0], 4 - step[0]) - min(step[1], 4 - step[1]) - 0.5 * step[2])

    def zdev(d):
        return dev(x, yh, yl, (z + d) % NZ, core)

    def odev(dy, dc):
        to_y, to_core = (y_at + dy) % 4, (core + dc) % 2
        return to_y, to_core, dev(x, to_y // 2, to_y % 2, z, to_core)

    def sdev(dx, dy, dc):
        to_y = (y_at + dy) % 4
        return dev((x + dx) % NX, to_y // 2, to_y % 2, z, (core + dc) % 2)

    def is_me(dest):
        return jnp.logical_and(jnp.logical_and(dest[0] == row, dest[1] == col), dest[2] == core)

    obs_copy = pltpu.make_async_copy(obs, obs_v, in_sem.at[0])
    w_copy = pltpu.make_async_copy(weights, w_v, in_sem.at[1])
    log_copy = pltpu.make_async_copy(logp, log_v, in_sem.at[3])
    log_copy.start()
    obs_copy.start()
    w_copy.start()

    def panel(comp, lo):
        start = pl.multiple_of((yh * 2 + lo) * NP, 128)
        return green.at[x, comp, :, pl.ds(start, NP)]

    lanes_of = [pl.ds(comp * NP, NP) for comp in range(2)]
    staged = []
    for comp in range(2):
        staged.append(pltpu.make_async_copy(panel(comp, yl), u.at[0, yl, 0, :, lanes_of[comp]], in_sem.at[4 + comp]))
        staged.append(pltpu.make_async_copy(panel(comp, other), away.at[:, lanes_of[comp]], in_sem.at[6 + comp]))
    for copy in staged:
        copy.start()

    def centre(zi, zj):
        delta = (zj - zi) % NZ
        from_i = jnp.where(delta >= 2, 1, 0)
        from_j = jnp.where(delta == 7, 0, jnp.where(delta == 4, 2, 1))
        zc = jnp.where(delta <= 3, zi + from_i, zj + from_j) % NZ
        return delta, zc

    def pair_dest(plane, zl):
        delta, zc = centre(2 * x + zl, z)
        swap = jnp.logical_or(delta == 0, delta >= 4)
        return delta, dev(plane, jnp.where(swap, yl, yh), jnp.where(swap, yh, yl), zc, core)

    pair_dests = []
    for plane in range(NX):
        for zl in range(2):
            pair_dests.append((plane, zl) + pair_dest(plane, zl))
    up = [dev(plane, yh, x // 2, z, core) for plane in range(NX)]
    down = [dev(2 * yl + k // 2, yh, k % 2, z, core) for k in range(4)]

    log_copy.wait()
    l_src[...] = jnp.zeros_like(l_src)
    for f in range(NX):
        l_src[f, :, 0:RUN] = log_v[0, f : f + 1, :]

    partner = dev(x, yh, other, z, core)
    diagonal = {d: dev(x, yh, other, (z + d) % NZ, core) for d in (1, -1)}
    y_near = [odev(dy, 0)[2] for dy in (1, 3)]
    across = dev(x, 1 - yh, other, z, core)
    sibling = dev(x, yh, yl, z, 1 - core)
    z_near = [zdev(d) for d in (1, -1, 2, -2)]
    xy_near = [dev((x + dx) % NX, yh, lo, z, core) for dx in (2, 1, 3) for lo in (other, yl)]
    near = xy_near + [diagonal[1], diagonal[-1], partner, across, sibling] + z_near
    barrier = pltpu.get_barrier_semaphore()
    for dest in near:
        pl.semaphore_signal(barrier, inc=1, device_id=dest, device_id_type=MESH)
    for copy in staged:
        copy.wait()
    pl.semaphore_wait(barrier, len(near))

    def pass_token(k, dests):
        for dest in dests:
            pl.semaphore_signal(tokens.at[k], inc=1, device_id=dest, device_id_type=MESH)


    def send(src, dst, s_sem, r_sem, dest):
        copy = pltpu.make_async_remote_copy(
            src_ref=src, dst_ref=dst, send_sem=s_sem, recv_sem=r_sem, device_id=dest, device_id_type=MESH
        )
        copy.start()
        return copy

    def send_or_keep(src, dst, s_sem, r_sem, dest):
        mine = is_me(dest)
        @pl.when(jnp.logical_not(mine))
        def _():
            send(src, dst, s_sem, r_sem, dest)
        @pl.when(mine)
        def _():
            pltpu.make_async_copy(src, dst, r_sem).start()

    def finish_send(src, s_sem, dest):
        @pl.when(jnp.logical_not(is_me(dest)))
        def _():
            wait_bytes(src, s_sem)

    slot = (x % 2) * 2 + yl
    for f in range(NX):
        send_or_keep(l_src.at[f], l_in.at[slot], ls_sem.at[f], lr_sem.at[0], up[f])

    def launch(k, comp, src, dst, dest):
        send(src, dst.at[:, lanes_of[comp]], gs_sem.at[comp, k], gr_sem.at[comp, k], dest)

    own = u.at[0, yl, 0]
    for comp in range(2):
        launch(1, comp, own.at[:, lanes_of[comp]], x_left.at[1, yl], zdev(1))
        launch(2, comp, own.at[:, lanes_of[comp]], u.at[1, yl, 0], zdev(-1))
        launch(0, comp, away.at[:, lanes_of[comp]], u.at[0, yl, 0], partner)
    for comp in range(2):
        launch(3, comp, away.at[:, lanes_of[comp]], x_left.at[1, yl], diagonal[1])
        launch(4, comp, away.at[:, lanes_of[comp]], u.at[1, yl, 0], diagonal[-1])

    def build_turned(lo, j):
        u[j, lo, 1, :, 0:NP] = -u[j, lo, 0, :, NP : 2 * NP]
        u[j, lo, 1, :, NP : 2 * NP] = u[j, lo, 0, :, 0:NP]

    def build_weighted(g, psd2):
        for lo in range(2):
            x_psd[g, lo] = (x_left[g, lo].astype(F32) * psd2).astype(BF16)

    def correlate(it, j):
        tiles = [k for k, pair in enumerate(PAIRS) if pair[1] == j]
        first = PAIRS[tiles[0]][0]
        left = x_psd[first : first + len(tiles)].reshape(len(tiles) * 2 * ST, 2 * NP)
        right = u[j].reshape(4 * ST, 2 * NP)
        product = lax.dot_general(left, right, (((1,), (1,)), ((), ())), preferred_element_type=F32)
        for k, tile in enumerate(tiles):
            block = product[k * 2 * ST : (k + 1) * 2 * ST].reshape(2, 2, 16, 128).astype(BF16)
            for half in range(2):
                c_part[it, half, tile] = block[:, half]

    def sum_sems(it, first, stage):
        k = stage if first == 0 else 5 + stage
        return ph_s.at[it, k], ph_r.at[it, k]

    def sum_tiles(it, first, last):
        tiles = pl.ds(first, last - first)
        s_sem, r_sem = sum_sems(it, first, 0)
        send(c_part.at[it, 1 - core, tiles], core_in.at[it, tiles], s_sem, r_sem, sibling)
        wait_bytes(core_in.at[it, tiles], r_sem)
        y_all[it, y_at, tiles] = (c_part[it, core, tiles].astype(F32) + core_in[it, tiles].astype(F32)).astype(BF16)
        s_sem, r_sem = sum_sems(it, first, 1)
        for dy in (2, 1, 3):
            send(y_all.at[it, y_at, tiles], y_all.at[it, y_at, tiles], s_sem, r_sem, odev(dy, 0)[2])

    def arrive(k, comp, dst):
        wait_bytes(dst.at[:, lanes_of[comp]], gr_sem.at[comp, k])

    def pass_on(half, at):
        for comp in range(2):
            piece = x_left.at[1, half]
            arrive(at, comp, piece)
            launch(at + 4, comp, piece.at[:, lanes_of[comp]], x_left.at[2, half], zdev(1))
            piece = u.at[1, half, 0]
            arrive(at + 1, comp, piece)
            launch(at + 5, comp, piece.at[:, lanes_of[comp]], u.at[2, half, 0], zdev(-1))

    pass_token(0, z_near)

    obs_copy.wait()
    w_copy.wait()
    for zl in range(2):
        w = w_v[:, zl * ST : (zl + 1) * ST].astype(F32)
        for f in range(NX):
            real = w * obs_v[f, 0, :, zl * ST : (zl + 1) * ST]
            imag = w * obs_v[f, 1, :, zl * ST : (zl + 1) * ST]
            msg[f, zl] = jnp.concatenate([real, imag, w, w], axis=1).astype(BF16)

    pl.semaphore_wait(tokens.at[0], len(z_near))
    pass_token(1, y_near)
    wait_bytes(l_in, lr_sem.at[0])
    for d in z_steps:
        send(l_in, l_z.at[z], ls2_sem.at[0], lr_sem.at[1], zdev(d))
    l_z[z] = l_in[...]
    pass_on(yl, 1)
    pass_on(other, 3)
    pl.semaphore_wait(tokens.at[1], len(y_near))
    for comp in range(2):
        arrive(0, comp, u.at[0, other, 0])
    for k, (plane, zl, delta, dest) in enumerate(pair_dests):
        send_or_keep(msg.at[plane, zl], e_in.at[delta], es_sem.at[k], er_sem.at[0], dest)
    for lo in range(2):
        x_left[0, lo] = u[0, lo, 0]
        build_turned(lo, 0)
        build_turned(lo, 1)

    wait_bytes(l_z.at[pl.ds(0, NZ - 1)], lr_sem.at[1])
    for zz in range(NZ):
        for k in range(4):
            l_rows[k * NZ + zz : k * NZ + zz + 1, :] = l_z[zz, k]
    point = lax.broadcasted_iota(jnp.int32, (128, NP), 1)
    run_of = lax.shift_right_logical(point * 2731, 16)
    spread = (point - run_of * RUN == lax.broadcasted_iota(jnp.int32, (128, NP), 0)).astype(F32)
    spread_rows = jnp.dot(l_rows[...], spread, precision=HIGHEST, preferred_element_type=F32)
    run_row = lax.shift_right_logical(lax.broadcasted_iota(jnp.int32, (32, NP), 1) * 2731, 16)
    log_field = jnp.sum(
        jnp.where(run_row == lax.broadcasted_iota(jnp.int32, (32, NP), 0), spread_rows, 0.0), axis=0, keepdims=True
    )
    psd = jnp.exp(log_field)
    psd2 = jnp.concatenate([psd, psd], axis=1)
    build_weighted(0, psd2)

    build_weighted(1, psd2)
    correlate(0, 0)
    correlate(0, 1)
    sum_tiles(0, 0, 3)

    for half, at in ((yl, 5), (other, 7)):
        for comp in range(2):
            arrive(at, comp, x_left.at[2, half])
            arrive(at + 1, comp, u.at[2, half, 0])
    for lo in range(2):
        build_turned(lo, 2)
    build_weighted(2, psd2)
    correlate(0, 2)

    def pair_terms():
        wait_bytes(e_in, er_sem.at[0])
        lane_at = lax.broadcasted_iota(jnp.int32, (ST, 128), 1)
        same = (lane_at % ST == lax.broadcasted_iota(jnp.int32, (ST, 128), 0)).astype(BF16)
        part_at = lane_at // ST

        def turned(block):
            full = lax.dot_general(block, same, (((0,), (0,)), ((), ())), preferred_element_type=F32)
            result = jnp.where(part_at == 0, full[0:ST], full[ST : 2 * ST])
            result = jnp.where(part_at == 2, full[2 * ST : 3 * ST], result)
            return jnp.where(part_at == 3, full[3 * ST : 4 * ST], result)

        def conj(block):
            block = block.astype(F32)
            return jnp.where(part_at == 1, -block, block)

        blocks = (
            conj(e_in[0]),
            turned(e_in[1]) + conj(e_in[7]),
            turned(e_in[2]) + conj(e_in[6]),
            turned(e_in[3]) + conj(e_in[5]),
            conj(e_in[4]),
        )
        for tile, block in enumerate(blocks):
            pair_rows[tile] = jnp.where(yl == 0, block, pltpu.roll(block, 64, 1))
        own_rows = pl.ds(pl.multiple_of(core * 16, 16), 16)
        pair_all[y_at] = pair_rows[:, own_rows, :].astype(BF16)
        for dy in (2, 1, 3):
            send(pair_all.at[y_at], pair_all.at[y_at], pt_sem.at[0], pt_sem.at[1], odev(dy, 0)[2])

    def pair_tiles():
        wait_bytes(pair_all.at[pl.ds(0, 3)], pt_sem.at[1])
        low = lax.broadcasted_iota(jnp.int32, (16, 128), 1) < 64
        for tile in range(len(PAIRS)):
            for hi in range(2):
                first = pair_all[2 * hi, tile].astype(F32)
                second = pair_all[2 * hi + 1, tile].astype(F32)
                d_all[tile, hi] = jnp.where(low, first, second)
                w_all[tile, hi] = jnp.where(low, pltpu.roll(first, 64, 1), pltpu.roll(second, 64, 1)) * QUAD

    def finish_phase(it, phase):
        if phase == 2:
            wait_bytes(g_all.at[it, pl.ds(0, NZ - 1)], ph_s.at[it, 2])
        elif phase == 3:
            wait_bytes(s_all.at[it, pl.ds(0, NS - 1)], ph_s.at[it, 3])
        elif phase == 4:
            wait_bytes(core_in.at[it], ph_s.at[it, 4])
        else:
            for part in ((0, 3), (3, 5)) if it == 0 else ((0, 5),):
                tiles = pl.ds(part[0], part[1] - part[0])
                left = core_in.at[it, tiles] if phase == 0 else y_all.at[it, pl.ds(0, 3), tiles]
                wait_bytes(left, sum_sems(it, part[0], phase)[0])

    def finish_start():
        for comp in range(2):
            for k in range(9):
                wait_bytes(x_left.at[1, 0, :, lanes_of[comp]], gs_sem.at[comp, k])
        for f in range(NX):
            finish_send(l_src.at[f], ls_sem.at[f], up[f])
        wait_bytes(l_z.at[pl.ds(0, NZ - 1)], ls2_sem.at[0])
        for k, (plane, zl, delta, dest) in enumerate(pair_dests):
            finish_send(msg.at[plane, zl], es_sem.at[k], dest)
        wait_bytes(pair_all.at[pl.ds(0, 3)], pt_sem.at[0])
        for phase in range(5):
            finish_phase(0, phase)

    def exchange_rest(it, psd):
        phase = lambda k: (ph_s.at[it, k], ph_r.at[it, k])
        sum_tiles(it, 3 if it == 0 else 0, 5)
        if it == 0:
            pair_terms()
            pair_tiles()
        else:
            finish_start()
        for part in ((0, 3), (3, 5)) if it == 0 else ((0, 5),):
            tiles = pl.ds(part[0], part[1] - part[0])
            wait_bytes(y_all.at[it, pl.ds(0, 3), tiles], sum_sems(it, part[0], 1)[1])
        total = y_all[it, 0].astype(F32)
        for k in range(1, 4):
            total = total + y_all[it, k].astype(F32)
        b_full[it, core] = (w_all[...] * total - d_all[...]).astype(BF16)
        s_sem, r_sem = phase(4)
        send(b_full.at[it, core], b_full.at[it, core], s_sem, r_sem, sibling)
        wait_bytes(core_in.at[it], r_sem)

        width = 384
        terms = []
        for c in range(2 * NP // width):
            lanes = slice(c * width, (c + 1) * width)
            term = jnp.zeros((1, width), F32)
            for g in range(3):
                tiles = [k for k, pair in enumerate(PAIRS) if pair[0] == g]
                first = PAIRS[tiles[0]][1]
                b = jnp.concatenate(
                    [
                        jnp.concatenate([b_full[it, half, tile, hi] for hi in range(2) for half in range(2)], axis=0)
                        for tile in tiles
                    ],
                    axis=1,
                )
                right = u[first : first + len(tiles), :, :, :, lanes].reshape(len(tiles) * 4 * ST, width)
                field = jnp.dot(b, right, preferred_element_type=F32)
                left = x_left[g, :, :, lanes].reshape(2 * ST, width).astype(F32)
                term = term + jnp.sum(left * field, axis=0, keepdims=True)
            terms.append(term)
        half = len(terms) // 2
        mine = jnp.concatenate([terms[k] + terms[half + k] for k in range(half)], axis=1)
        g_mine[it] = mine
        s_sem, r_sem = phase(2)
        for d in z_steps:
            send(g_mine.at[it], g_all.at[it, z], s_sem, r_sem, zdev(d))
        g_all[it, z] = mine
        wait_bytes(g_all.at[it, pl.ds(0, NZ - 1)], r_sem)
        summed = g_all[it, 0]
        for k in range(1, NZ):
            summed = summed + g_all[it, k]
        return QUAD * psd * summed

    def start_mean(it, gradient):
        squares = gradient[:, 0:128] * gradient[:, 0:128]
        for k in range(1, NP // 128):
            squares = squares + gradient[:, k * 128 : (k + 1) * 128] * gradient[:, k * 128 : (k + 1) * 128]
        s_mine[it] = squares
        for step in s_steps:
            send(s_mine.at[it], s_all.at[it, mine_at], ph_s.at[it, 3], ph_r.at[it, 3], sdev(*step))
        s_all[it, mine_at] = squares

    def finish_mean(it):
        wait_bytes(s_all.at[it, pl.ds(0, NS - 1)], ph_r.at[it, 3])
        total = jnp.sum(jnp.sum(s_all[it], axis=0), axis=1, keepdims=True)
        return jnp.sqrt(total / ENTRIES + EPSILON)

    gradient = exchange_rest(0, psd)
    start_mean(0, gradient)
    log_field = log_field - DESCENT * gradient / finish_mean(0)

    psd = jnp.exp(log_field)
    psd2 = jnp.concatenate([psd, psd], axis=1)
    for g in range(3):
        build_weighted(g, psd2)
    for j in range(3):
        correlate(1, j)
    m_mine[...] = log_field
    for k in range(4):
        send_or_keep(m_mine, m_in.at[x], ms_sem.at[k], mr_sem.at[0], down[k])
    gradient = exchange_rest(1, psd)
    start_mean(1, gradient)
    o_mine[...] = gradient
    for k in range(4):
        send_or_keep(o_mine, o_in.at[x], os_sem.at[k], or_sem.at[0], down[k])

    start = (slot * NZ + z) * RUN
    pick = (
        lax.broadcasted_iota(jnp.int32, (NP, 128), 0) == lax.broadcasted_iota(jnp.int32, (NP, 128), 1) + start
    ).astype(F32)

    def run_of_points(rows, parts):
        rows[...] = jnp.zeros_like(rows)
        for f in range(NX):
            rows[f : f + 1, :] = parts[f]
        return jnp.dot(rows[...], pick, precision=HIGHEST, preferred_element_type=F32)[0:NX, 0:RUN]

    wait_bytes(m_in, mr_sem.at[0])
    own_field = run_of_points(rows_m, m_in)
    wait_bytes(o_in, or_sem.at[0])
    own_gradient = run_of_points(rows_o, o_in)
    out[0] = own_field - DESCENT * own_gradient / finish_mean(1)

    for phase in range(5):
        finish_phase(1, phase)
    for k in range(4):
        finish_send(m_mine, ms_sem.at[k], down[k])
        finish_send(o_mine, os_sem.at[k], down[k])


def body(green_panel, log_psd, observed, pair_weights):
    vmem = pltpu.VMEM
    dma = pltpu.SemaphoreType.DMA
    return pl.pallas_call(
        kernel,
        out_shape=jax.ShapeDtypeStruct(log_psd.shape, F32),
        in_specs=[
            pl.BlockSpec(memory_space=pltpu.HBM),
            pl.BlockSpec(memory_space=pltpu.HBM),
            pl.BlockSpec(memory_space=pltpu.HBM),
            pl.BlockSpec(memory_space=pltpu.HBM),
        ],
        out_specs=pl.BlockSpec(memory_space=pltpu.VMEM),
        scratch_shapes=[
            vmem((3, 2, 2, ST, 2 * NP), BF16),
            vmem((3, 2, ST, 2 * NP), BF16),
            vmem((3, 2, ST, 2 * NP), BF16),
            vmem((ST, 2 * NP), BF16),
            vmem((1, NX, RUN), F32),
            vmem((NX, 2, ST, 2 * ST), F32),
            vmem((ST, 2 * ST), jnp.int32),
            vmem((NX, 2, ST, 128), BF16),
            vmem((NZ, ST, 128), BF16),
            vmem((5, 2, 16, 128), F32),
            vmem((5, 2, 16, 128), F32),
            vmem((NX, 1, 128), F32),
            vmem((4, 1, 128), F32),
            vmem((NZ, 4, 1, 128), F32),
            vmem((32, 128), F32),
            vmem((5, ST, 128), F32),
            vmem((4, 5, 16, 128), BF16),
            vmem((ITERS, 2, 5, 2, 16, 128), BF16),
            vmem((ITERS, 5, 2, 16, 128), BF16),
            vmem((ITERS, 4, 5, 2, 16, 128), BF16),
            vmem((ITERS, 2, 5, 2, 16, 128), BF16),
            vmem((ITERS, 1, NP), F32),
            vmem((ITERS, NZ, 1, NP), F32),
            vmem((ITERS, 1, 128), F32),
            vmem((ITERS, NS, 1, 128), F32),
            vmem((1, NP), F32),
            vmem((1, NP), F32),
            vmem((NX, 1, NP), F32),
            vmem((NX, 1, NP), F32),
            vmem((8, NP), F32),
            vmem((8, NP), F32),
            dma((8,)),
            dma((2, 9)),
            dma((2, 9)),
            dma((1,)),
            dma((8,)),
            dma((2,)),
            dma((4,)),
            dma((1,)),
            pltpu.SemaphoreType.REGULAR((2,)),
            dma((2,)),
            dma((ITERS, 7)),
            dma((ITERS, 7)),
            dma((1,)),
            dma((4,)),
            dma((1,)),
            dma((4,)),
        ],
        compiler_params=pltpu.CompilerParams(
            collective_id=0, has_side_effects=True, vmem_limit_bytes=63 * 1024 * 1024
        ),
    )(green_panel, log_psd, jnp.swapaxes(observed, 2, 3), pair_weights.T)


def solution(mesh):
    return jax.shard_map(
        body,
        mesh=mesh,
        in_specs=(
            P(None, None, "col", "pts"),
            P("pts", None, ("row", "col")),
            P(None, None, "row", "col"),
            P("row", "col"),
        ),
        out_specs=P("pts", None, ("row", "col")),
        check_vma=False,
    )
```

```python
import functools

import jax
import jax.numpy as jnp
from jax import lax
from jax.experimental import pallas as pl
from jax.experimental.pallas import tpu as pltpu
from jax.sharding import PartitionSpec as P

MESH = pl.DeviceIdType.MESH
HIGHEST = lax.Precision.HIGHEST
F32 = jnp.float32
BF16 = jnp.bfloat16

ITERS = 2
NX = 4
NZ = 8
NO = 8
NS = NX * NO
ST = 32
NP = 768
RUN = 24
ENTRIES = 4 * 6144
QUAD = 1.0 / 6144
EPSILON = 1e-06
DESCENT = 0.1

PAIRS = ((0, 0), (0, 1), (1, 1), (1, 2), (2, 2))


def wait_bytes(ref, sem):
    pltpu.make_async_copy(ref, ref, sem).wait()


def kernel(
    green, logp, obs, weights, out,
    u, x_left, x_psd, away, log_v, obs_v, w_v, msg, e_in, d_all, w_all,
    l_src, l_in, l_z, l_rows, pair_rows, pair_all, c_part, core_in, y_all, b_full, g_mine, g_all, s_mine, s_all,
    m_mine, o_mine, m_in, o_in, rows_m, rows_o,
    in_sem, gr_sem, gs_sem, er_sem, es_sem, lr_sem, ls_sem, ls2_sem,
    tokens, pt_sem, ph_r, ph_s, mr_sem, ms_sem, or_sem, os_sem,
):
    row = lax.axis_index("row")
    col = lax.axis_index("col")
    core = lax.axis_index("pts")
    yh, x = row // 4, row % 4
    yl, z = col // 8, col % 8
    mine_at = x * NO + yh * 4 + yl * 2 + core
    other = 1 - yl

    def dev(x_, yh_, yl_, z_, core_):
        return (yh_ * 4 + x_, yl_ * 8 + z_, core_)

    z_steps = (4, 3, 5, 2, 6, 1, 7)
    y_at = yh * 2 + yl
    o_steps = [(dy, dc) for dy in (2, 1, 3, 0) for dc in (1, 0) if dy or dc]
    s_steps = [(dx, dy, dc) for dx in (2, 1, 3, 0) for dy in (2, 1, 3, 0) for dc in (1, 0) if dx or dy or dc]
    s_steps.sort(key=lambda step: -min(step[0], 4 - step[0]) - min(step[1], 4 - step[1]) - 0.5 * step[2])

    def zdev(d):
        return dev(x, yh, yl, (z + d) % NZ, core)

    def odev(dy, dc):
        to_y, to_core = (y_at + dy) % 4, (core + dc) % 2
        return to_y, to_core, dev(x, to_y // 2, to_y % 2, z, to_core)

    def sdev(dx, dy, dc):
        to_y = (y_at + dy) % 4
        return dev((x + dx) % NX, to_y // 2, to_y % 2, z, (core + dc) % 2)

    def is_me(dest):
        return jnp.logical_and(jnp.logical_and(dest[0] == row, dest[1] == col), dest[2] == core)

    obs_copy = pltpu.make_async_copy(obs, obs_v, in_sem.at[0])
    w_copy = pltpu.make_async_copy(weights, w_v, in_sem.at[1])
    log_copy = pltpu.make_async_copy(logp, log_v, in_sem.at[3])
    log_copy.start()
    obs_copy.start()
    w_copy.start()

    def panel(comp, lo):
        start = pl.multiple_of((yh * 2 + lo) * NP, 128)
        return green.at[x, comp, :, pl.ds(start, NP)]

    lanes_of = [pl.ds(comp * NP, NP) for comp in range(2)]
    staged = []
    for comp in range(2):
        staged.append(pltpu.make_async_copy(panel(comp, yl), u.at[0, yl, 0, :, lanes_of[comp]], in_sem.at[4 + comp]))
        staged.append(pltpu.make_async_copy(panel(comp, other), away.at[:, lanes_of[comp]], in_sem.at[6 + comp]))
    for copy in staged:
        copy.start()

    def centre(zi, zj):
        delta = (zj - zi) % NZ
        from_i = jnp.where(delta >= 2, 1, 0)
        from_j = jnp.where(delta == 7, 0, jnp.where(delta == 4, 2, 1))
        zc = jnp.where(delta <= 3, zi + from_i, zj + from_j) % NZ
        return delta, zc

    core_rows = pl.ds(pl.multiple_of(core * 16, 16), 16)

    def as_it_is(delta):
        return jnp.logical_or(delta == 0, delta >= 4)

    def pair_dest(plane, zl):
        delta, zc = centre(2 * x + zl, z)
        swap = as_it_is(delta)
        return delta, dev(plane, jnp.where(swap, yl, yh), jnp.where(swap, yh, yl), zc, core)

    pair_dests = []
    for plane in range(NX):
        for zl in range(2):
            pair_dests.append((plane, zl) + pair_dest(plane, zl))
    up = [dev(plane, yh, x // 2, z, core) for plane in range(NX)]
    down = [dev(2 * yl + k // 2, yh, k % 2, z, core) for k in range(4)]

    log_copy.wait()
    l_src[...] = jnp.zeros_like(l_src)
    e_in[...] = jnp.zeros_like(e_in)
    for f in range(NX):
        l_src[f, :, 0:RUN] = log_v[0, f : f + 1, :]

    partner = dev(x, yh, other, z, core)
    diagonal = {d: dev(x, yh, other, (z + d) % NZ, core) for d in (1, -1)}
    y_near = [odev(dy, 0)[2] for dy in (1, 3)]
    across = dev(x, 1 - yh, other, z, core)
    sibling = dev(x, yh, yl, z, 1 - core)
    z_near = [zdev(d) for d in (1, -1, 2, -2)]
    xy_near = [dev((x + dx) % NX, yh, lo, z, core) for dx in (2, 1, 3) for lo in (other, yl)]
    near = xy_near + [diagonal[1], diagonal[-1], partner, across, sibling] + z_near
    barrier = pltpu.get_barrier_semaphore()
    for dest in near:
        pl.semaphore_signal(barrier, inc=1, device_id=dest, device_id_type=MESH)
    for copy in staged:
        copy.wait()
    pl.semaphore_wait(barrier, len(near))

    def pass_token(k, dests):
        for dest in dests:
            pl.semaphore_signal(tokens.at[k], inc=1, device_id=dest, device_id_type=MESH)


    def send(src, dst, s_sem, r_sem, dest):
        copy = pltpu.make_async_remote_copy(
            src_ref=src, dst_ref=dst, send_sem=s_sem, recv_sem=r_sem, device_id=dest, device_id_type=MESH
        )
        copy.start()
        return copy

    def send_or_keep(src, dst, s_sem, r_sem, dest):
        mine = is_me(dest)
        @pl.when(jnp.logical_not(mine))
        def _():
            send(src, dst, s_sem, r_sem, dest)
        @pl.when(mine)
        def _():
            pltpu.make_async_copy(src, dst, r_sem).start()

    def finish_send(src, s_sem, dest):
        @pl.when(jnp.logical_not(is_me(dest)))
        def _():
            wait_bytes(src, s_sem)

    slot = (x % 2) * 2 + yl
    for f in range(NX):
        send_or_keep(l_src.at[f], l_in.at[slot], ls_sem.at[f], lr_sem.at[0], up[f])

    def launch(k, comp, src, dst, dest):
        send(src, dst.at[:, lanes_of[comp]], gs_sem.at[comp, k], gr_sem.at[comp, k], dest)

    own = u.at[0, yl, 0]
    for comp in range(2):
        launch(1, comp, own.at[:, lanes_of[comp]], x_left.at[1, yl], zdev(1))
        launch(2, comp, own.at[:, lanes_of[comp]], u.at[1, yl, 0], zdev(-1))
        launch(0, comp, away.at[:, lanes_of[comp]], u.at[0, yl, 0], partner)
    for comp in range(2):
        launch(3, comp, away.at[:, lanes_of[comp]], x_left.at[1, yl], diagonal[1])
        launch(4, comp, away.at[:, lanes_of[comp]], u.at[1, yl, 0], diagonal[-1])

    def build_turned(lo, j):
        u[j, lo, 1, :, 0:NP] = -u[j, lo, 0, :, NP : 2 * NP]
        u[j, lo, 1, :, NP : 2 * NP] = u[j, lo, 0, :, 0:NP]

    def build_weighted(g, psd2):
        for lo in range(2):
            x_psd[g, lo] = (x_left[g, lo].astype(F32) * psd2).astype(BF16)

    def correlate(it, j):
        tiles = [k for k, pair in enumerate(PAIRS) if pair[1] == j]
        first = PAIRS[tiles[0]][0]
        left = x_psd[first : first + len(tiles)].reshape(len(tiles) * 2 * ST, 2 * NP)
        right = u[j].reshape(4 * ST, 2 * NP)
        product = lax.dot_general(left, right, (((1,), (1,)), ((), ())), preferred_element_type=F32)
        for k, tile in enumerate(tiles):
            block = product[k * 2 * ST : (k + 1) * 2 * ST].reshape(2, 2, 16, 128).astype(BF16)
            for half in range(2):
                c_part[it, half, tile] = block[:, half]

    def sum_sems(it, first, stage):
        k = stage if first == 0 else 5 + stage
        return ph_s.at[it, k], ph_r.at[it, k]

    def sum_tiles(it, first, last):
        tiles = pl.ds(first, last - first)
        s_sem, r_sem = sum_sems(it, first, 0)
        send(c_part.at[it, 1 - core, tiles], core_in.at[it, tiles], s_sem, r_sem, sibling)
        wait_bytes(core_in.at[it, tiles], r_sem)
        y_all[it, y_at, tiles] = (c_part[it, core, tiles].astype(F32) + core_in[it, tiles].astype(F32)).astype(BF16)
        s_sem, r_sem = sum_sems(it, first, 1)
        for dy in (2, 1, 3):
            send(y_all.at[it, y_at, tiles], y_all.at[it, y_at, tiles], s_sem, r_sem, odev(dy, 0)[2])

    def arrive(k, comp, dst):
        wait_bytes(dst.at[:, lanes_of[comp]], gr_sem.at[comp, k])

    def pass_on(half, at):
        for comp in range(2):
            piece = x_left.at[1, half]
            arrive(at, comp, piece)
            launch(at + 4, comp, piece.at[:, lanes_of[comp]], x_left.at[2, half], zdev(1))
            piece = u.at[1, half, 0]
            arrive(at + 1, comp, piece)
            launch(at + 5, comp, piece.at[:, lanes_of[comp]], u.at[2, half, 0], zdev(-1))

    pass_token(0, z_near)

    obs_copy.wait()
    w_copy.wait()
    for zl in range(2):
        w = w_v[:, zl * ST : (zl + 1) * ST].astype(F32)
        for f in range(NX):
            real = w * obs_v[f, 0, :, zl * ST : (zl + 1) * ST]
            imag = w * obs_v[f, 1, :, zl * ST : (zl + 1) * ST]
            msg[f, zl] = jnp.concatenate([real, imag, w, w], axis=1).astype(BF16)

    pl.semaphore_wait(tokens.at[0], len(z_near))
    pass_token(1, y_near)
    wait_bytes(l_in, lr_sem.at[0])
    for d in z_steps:
        send(l_in, l_z.at[z], ls2_sem.at[0], lr_sem.at[1], zdev(d))
    l_z[z] = l_in[...]
    pass_on(yl, 1)
    pass_on(other, 3)
    pl.semaphore_wait(tokens.at[1], len(y_near))
    for comp in range(2):
        arrive(0, comp, u.at[0, other, 0])
    for k, (plane, zl, delta, dest) in enumerate(pair_dests):
        block = msg.at[plane, zl]

        @pl.when(as_it_is(delta))
        def _(block=block, delta=delta, k=k, dest=dest):
            send_or_keep(block.at[core_rows], e_in.at[delta, core_rows], es_sem.at[k], er_sem.at[0], dest)

        @pl.when(jnp.logical_not(as_it_is(delta)))
        def _(block=block, delta=delta, k=k, dest=dest):
            send(block, e_in.at[delta], es_sem.at[k], er_sem.at[1], dest)

    for lo in range(2):
        x_left[0, lo] = u[0, lo, 0]
        build_turned(lo, 0)
        build_turned(lo, 1)

    wait_bytes(l_z.at[pl.ds(0, NZ - 1)], lr_sem.at[1])
    for zz in range(NZ):
        for k in range(4):
            l_rows[k * NZ + zz : k * NZ + zz + 1, :] = l_z[zz, k]
    point = lax.broadcasted_iota(jnp.int32, (128, NP), 1)
    run_of = lax.shift_right_logical(point * 2731, 16)
    spread = (point - run_of * RUN == lax.broadcasted_iota(jnp.int32, (128, NP), 0)).astype(F32)
    spread_rows = jnp.dot(l_rows[...], spread, precision=HIGHEST, preferred_element_type=F32)
    run_row = lax.shift_right_logical(lax.broadcasted_iota(jnp.int32, (32, NP), 1) * 2731, 16)
    log_field = jnp.sum(
        jnp.where(run_row == lax.broadcasted_iota(jnp.int32, (32, NP), 0), spread_rows, 0.0), axis=0, keepdims=True
    )
    psd = jnp.exp(log_field)
    psd2 = jnp.concatenate([psd, psd], axis=1)
    build_weighted(0, psd2)

    build_weighted(1, psd2)
    correlate(0, 0)
    correlate(0, 1)
    sum_tiles(0, 0, 3)

    for half, at in ((yl, 5), (other, 7)):
        for comp in range(2):
            arrive(at, comp, x_left.at[2, half])
            arrive(at + 1, comp, u.at[2, half, 0])
    for lo in range(2):
        build_turned(lo, 2)
    build_weighted(2, psd2)
    correlate(0, 2)

    def pair_terms():
        wait_bytes(e_in.at[pl.ds(0, 5), pl.ds(0, 16)], er_sem.at[0])
        wait_bytes(e_in.at[pl.ds(0, 3)], er_sem.at[1])
        lane_at = lax.broadcasted_iota(jnp.int32, (ST, 128), 1)
        same = (lane_at % ST == lax.broadcasted_iota(jnp.int32, (ST, 128), 0)).astype(BF16)
        part_at = lane_at // ST

        def turned(block):
            full = lax.dot_general(block, same, (((0,), (0,)), ((), ())), preferred_element_type=F32)
            result = jnp.where(part_at == 0, full[0:ST], full[ST : 2 * ST])
            result = jnp.where(part_at == 2, full[2 * ST : 3 * ST], result)
            return jnp.where(part_at == 3, full[3 * ST : 4 * ST], result)

        def conj(block):
            block = block.astype(F32)
            return jnp.where(part_at == 1, -block, block)

        blocks = (
            conj(e_in[0]),
            turned(e_in[1]) + conj(e_in[7]),
            turned(e_in[2]) + conj(e_in[6]),
            turned(e_in[3]) + conj(e_in[5]),
            conj(e_in[4]),
        )
        for tile, block in enumerate(blocks):
            pair_rows[tile] = jnp.where(yl == 0, block, pltpu.roll(block, 64, 1))
        pair_all[y_at] = pair_rows[:, core_rows, :].astype(BF16)
        for dy in (2, 1, 3):
            send(pair_all.at[y_at], pair_all.at[y_at], pt_sem.at[0], pt_sem.at[1], odev(dy, 0)[2])

    def pair_tiles():
        wait_bytes(pair_all.at[pl.ds(0, 3)], pt_sem.at[1])
        low = lax.broadcasted_iota(jnp.int32, (16, 128), 1) < 64
        for tile in range(len(PAIRS)):
            for hi in range(2):
                first = pair_all[2 * hi, tile].astype(F32)
                second = pair_all[2 * hi + 1, tile].astype(F32)
                d_all[tile, hi] = jnp.where(low, first, second)
                w_all[tile, hi] = jnp.where(low, pltpu.roll(first, 64, 1), pltpu.roll(second, 64, 1)) * QUAD

    def finish_phase(it, phase):
        if phase == 2:
            wait_bytes(g_all.at[it, pl.ds(0, NZ - 1)], ph_s.at[it, 2])
        elif phase == 3:
            wait_bytes(s_all.at[it, pl.ds(0, NS - 1)], ph_s.at[it, 3])
        elif phase == 4:
            wait_bytes(core_in.at[it], ph_s.at[it, 4])
        else:
            for part in ((0, 3), (3, 5)) if it == 0 else ((0, 5),):
                tiles = pl.ds(part[0], part[1] - part[0])
                left = core_in.at[it, tiles] if phase == 0 else y_all.at[it, pl.ds(0, 3), tiles]
                wait_bytes(left, sum_sems(it, part[0], phase)[0])

    def finish_start():
        for comp in range(2):
            for k in range(9):
                wait_bytes(x_left.at[1, 0, :, lanes_of[comp]], gs_sem.at[comp, k])
        for f in range(NX):
            finish_send(l_src.at[f], ls_sem.at[f], up[f])
        wait_bytes(l_z.at[pl.ds(0, NZ - 1)], ls2_sem.at[0])
        for k, (plane, zl, delta, dest) in enumerate(pair_dests):
            @pl.when(as_it_is(delta))
            def _(block=msg.at[plane, zl, core_rows], k=k, dest=dest):
                finish_send(block, es_sem.at[k], dest)

            @pl.when(jnp.logical_not(as_it_is(delta)))
            def _(block=msg.at[plane, zl], k=k):
                wait_bytes(block, es_sem.at[k])

        wait_bytes(pair_all.at[pl.ds(0, 3)], pt_sem.at[0])
        for phase in range(5):
            finish_phase(0, phase)

    def exchange_rest(it, psd):
        phase = lambda k: (ph_s.at[it, k], ph_r.at[it, k])
        sum_tiles(it, 3 if it == 0 else 0, 5)
        if it == 0:
            pair_terms()
            pair_tiles()
        else:
            finish_start()
        for part in ((0, 3), (3, 5)) if it == 0 else ((0, 5),):
            tiles = pl.ds(part[0], part[1] - part[0])
            wait_bytes(y_all.at[it, pl.ds(0, 3), tiles], sum_sems(it, part[0], 1)[1])
        total = y_all[it, 0].astype(F32)
        for k in range(1, 4):
            total = total + y_all[it, k].astype(F32)
        b_full[it, core] = (w_all[...] * total - d_all[...]).astype(BF16)
        s_sem, r_sem = phase(4)
        send(b_full.at[it, core], b_full.at[it, core], s_sem, r_sem, sibling)
        wait_bytes(core_in.at[it], r_sem)

        width = 384
        terms = []
        for c in range(2 * NP // width):
            lanes = slice(c * width, (c + 1) * width)
            term = jnp.zeros((1, width), F32)
            for g in range(3):
                tiles = [k for k, pair in enumerate(PAIRS) if pair[0] == g]
                first = PAIRS[tiles[0]][1]
                b = jnp.concatenate(
                    [
                        jnp.concatenate([b_full[it, half, tile, hi] for hi in range(2) for half in range(2)], axis=0)
                        for tile in tiles
                    ],
                    axis=1,
                )
                right = u[first : first + len(tiles), :, :, :, lanes].reshape(len(tiles) * 4 * ST, width)
                field = jnp.dot(b, right, preferred_element_type=F32)
                left = x_left[g, :, :, lanes].reshape(2 * ST, width).astype(F32)
                term = term + jnp.sum(left * field, axis=0, keepdims=True)
            terms.append(term)
        half = len(terms) // 2
        mine = jnp.concatenate([terms[k] + terms[half + k] for k in range(half)], axis=1)
        g_mine[it] = mine
        s_sem, r_sem = phase(2)
        for d in z_steps:
            send(g_mine.at[it], g_all.at[it, z], s_sem, r_sem, zdev(d))
        g_all[it, z] = mine
        wait_bytes(g_all.at[it, pl.ds(0, NZ - 1)], r_sem)
        summed = g_all[it, 0]
        for k in range(1, NZ):
            summed = summed + g_all[it, k]
        return QUAD * psd * summed

    def start_mean(it, gradient):
        squares = gradient[:, 0:128] * gradient[:, 0:128]
        for k in range(1, NP // 128):
            squares = squares + gradient[:, k * 128 : (k + 1) * 128] * gradient[:, k * 128 : (k + 1) * 128]
        s_mine[it] = squares
        for step in s_steps:
            send(s_mine.at[it], s_all.at[it, mine_at], ph_s.at[it, 3], ph_r.at[it, 3], sdev(*step))
        s_all[it, mine_at] = squares

    def finish_mean(it):
        wait_bytes(s_all.at[it, pl.ds(0, NS - 1)], ph_r.at[it, 3])
        total = jnp.sum(jnp.sum(s_all[it], axis=0), axis=1, keepdims=True)
        return jnp.sqrt(total / ENTRIES + EPSILON)

    gradient = exchange_rest(0, psd)
    start_mean(0, gradient)
    log_field = log_field - DESCENT * gradient / finish_mean(0)

    psd = jnp.exp(log_field)
    psd2 = jnp.concatenate([psd, psd], axis=1)
    for g in range(3):
        build_weighted(g, psd2)
    for j in range(3):
        correlate(1, j)
    m_mine[...] = log_field
    for k in range(4):
        send_or_keep(m_mine, m_in.at[x], ms_sem.at[k], mr_sem.at[0], down[k])
    gradient = exchange_rest(1, psd)
    start_mean(1, gradient)
    o_mine[...] = gradient
    for k in range(4):
        send_or_keep(o_mine, o_in.at[x], os_sem.at[k], or_sem.at[0], down[k])

    start = (slot * NZ + z) * RUN
    pick = (
        lax.broadcasted_iota(jnp.int32, (NP, 128), 0) == lax.broadcasted_iota(jnp.int32, (NP, 128), 1) + start
    ).astype(F32)

    def run_of_points(rows, parts):
        rows[...] = jnp.zeros_like(rows)
        for f in range(NX):
            rows[f : f + 1, :] = parts[f]
        return jnp.dot(rows[...], pick, precision=HIGHEST, preferred_element_type=F32)[0:NX, 0:RUN]

    wait_bytes(m_in, mr_sem.at[0])
    own_field = run_of_points(rows_m, m_in)
    wait_bytes(o_in, or_sem.at[0])
    own_gradient = run_of_points(rows_o, o_in)
    out[0] = own_field - DESCENT * own_gradient / finish_mean(1)

    for phase in range(5):
        finish_phase(1, phase)
    for k in range(4):
        finish_send(m_mine, ms_sem.at[k], down[k])
        finish_send(o_mine, os_sem.at[k], down[k])


def body(green_panel, log_psd, observed, pair_weights):
    vmem = pltpu.VMEM
    dma = pltpu.SemaphoreType.DMA
    return pl.pallas_call(
        kernel,
        out_shape=jax.ShapeDtypeStruct(log_psd.shape, F32),
        in_specs=[
            pl.BlockSpec(memory_space=pltpu.HBM),
            pl.BlockSpec(memory_space=pltpu.HBM),
            pl.BlockSpec(memory_space=pltpu.HBM),
            pl.BlockSpec(memory_space=pltpu.HBM),
        ],
        out_specs=pl.BlockSpec(memory_space=pltpu.VMEM),
        scratch_shapes=[
            vmem((3, 2, 2, ST, 2 * NP), BF16),
            vmem((3, 2, ST, 2 * NP), BF16),
            vmem((3, 2, ST, 2 * NP), BF16),
            vmem((ST, 2 * NP), BF16),
            vmem((1, NX, RUN), F32),
            vmem((NX, 2, ST, 2 * ST), F32),
            vmem((ST, 2 * ST), jnp.int32),
            vmem((NX, 2, ST, 128), BF16),
            vmem((NZ, ST, 128), BF16),
            vmem((5, 2, 16, 128), F32),
            vmem((5, 2, 16, 128), F32),
            vmem((NX, 1, 128), F32),
            vmem((4, 1, 128), F32),
            vmem((NZ, 4, 1, 128), F32),
            vmem((32, 128), F32),
            vmem((5, ST, 128), F32),
            vmem((4, 5, 16, 128), BF16),
            vmem((ITERS, 2, 5, 2, 16, 128), BF16),
            vmem((ITERS, 5, 2, 16, 128), BF16),
            vmem((ITERS, 4, 5, 2, 16, 128), BF16),
            vmem((ITERS, 2, 5, 2, 16, 128), BF16),
            vmem((ITERS, 1, NP), F32),
            vmem((ITERS, NZ, 1, NP), F32),
            vmem((ITERS, 1, 128), F32),
            vmem((ITERS, NS, 1, 128), F32),
            vmem((1, NP), F32),
            vmem((1, NP), F32),
            vmem((NX, 1, NP), F32),
            vmem((NX, 1, NP), F32),
            vmem((8, NP), F32),
            vmem((8, NP), F32),
            dma((8,)),
            dma((2, 9)),
            dma((2, 9)),
            dma((2,)),
            dma((8,)),
            dma((2,)),
            dma((4,)),
            dma((1,)),
            pltpu.SemaphoreType.REGULAR((2,)),
            dma((2,)),
            dma((ITERS, 7)),
            dma((ITERS, 7)),
            dma((1,)),
            dma((4,)),
            dma((1,)),
            dma((4,)),
        ],
        compiler_params=pltpu.CompilerParams(
            collective_id=0, has_side_effects=True, vmem_limit_bytes=63 * 1024 * 1024
        ),
    )(green_panel, log_psd, jnp.swapaxes(observed, 2, 3), pair_weights.T)


def solution(mesh):
    return jax.shard_map(
        body,
        mesh=mesh,
        in_specs=(
            P(None, None, "col", "pts"),
            P("pts", None, ("row", "col")),
            P(None, None, "row", "col"),
            P("row", "col"),
        ),
        out_specs=P("pts", None, ("row", "col")),
        check_vma=False,
    )
```

```python
import functools

import jax
import jax.numpy as jnp
from jax import lax
from jax.experimental import pallas as pl
from jax.experimental.pallas import tpu as pltpu
from jax.sharding import PartitionSpec as P

MESH = pl.DeviceIdType.MESH
HIGHEST = lax.Precision.HIGHEST
F32 = jnp.float32
BF16 = jnp.bfloat16

ITERS = 2
NX = 4
NZ = 8
NO = 8
NS = NX * NO
ST = 32
NP = 768
RUN = 24
ENTRIES = 4 * 6144
QUAD = 1.0 / 6144
EPSILON = 1e-06
DESCENT = 0.1

PAIRS = ((0, 0), (0, 1), (1, 1), (1, 2), (2, 2))


def wait_bytes(ref, sem):
    pltpu.make_async_copy(ref, ref, sem).wait()


def kernel(
    green, logp, obs, weights, out,
    u, x_left, x_psd, away, log_v, obs_v, w_v, msg, e_in, d_all, w_all,
    l_src, l_in, l_z, l_rows, pair_all, c_part, core_in, y_all, b_full, g_mine, g_all, s_mine, s_all,
    m_mine, o_mine, m_in, o_in, rows_m, rows_o,
    in_sem, gr_sem, gs_sem, er_sem, es_sem, lr_sem, ls_sem, ls2_sem,
    tokens, pt_sem, ph_r, ph_s, mr_sem, ms_sem, or_sem, os_sem,
):
    row = lax.axis_index("row")
    col = lax.axis_index("col")
    core = lax.axis_index("pts")
    yh, x = row // 4, row % 4
    yl, z = col // 8, col % 8
    mine_at = x * NO + yh * 4 + yl * 2 + core
    other = 1 - yl

    def dev(x_, yh_, yl_, z_, core_):
        return (yh_ * 4 + x_, yl_ * 8 + z_, core_)

    z_steps = (4, 3, 5, 2, 6, 1, 7)
    y_at = yh * 2 + yl
    o_steps = [(dy, dc) for dy in (2, 1, 3, 0) for dc in (1, 0) if dy or dc]
    s_steps = [(dx, dy, dc) for dx in (2, 1, 3, 0) for dy in (2, 1, 3, 0) for dc in (1, 0) if dx or dy or dc]
    s_steps.sort(key=lambda step: -min(step[0], 4 - step[0]) - min(step[1], 4 - step[1]) - 0.5 * step[2])

    def zdev(d):
        return dev(x, yh, yl, (z + d) % NZ, core)

    def odev(dy, dc):
        to_y, to_core = (y_at + dy) % 4, (core + dc) % 2
        return to_y, to_core, dev(x, to_y // 2, to_y % 2, z, to_core)

    def sdev(dx, dy, dc):
        to_y = (y_at + dy) % 4
        return dev((x + dx) % NX, to_y // 2, to_y % 2, z, (core + dc) % 2)

    def is_me(dest):
        return jnp.logical_and(jnp.logical_and(dest[0] == row, dest[1] == col), dest[2] == core)

    obs_copy = pltpu.make_async_copy(obs, obs_v, in_sem.at[0])
    w_copy = pltpu.make_async_copy(weights, w_v, in_sem.at[1])
    log_copy = pltpu.make_async_copy(logp, log_v, in_sem.at[3])
    log_copy.start()
    obs_copy.start()
    w_copy.start()

    def panel(comp, lo):
        start = pl.multiple_of((yh * 2 + lo) * NP, 128)
        return green.at[x, comp, :, pl.ds(start, NP)]

    lanes_of = [pl.ds(comp * NP, NP) for comp in range(2)]
    staged = []
    for comp in range(2):
        staged.append(pltpu.make_async_copy(panel(comp, yl), u.at[0, yl, 0, :, lanes_of[comp]], in_sem.at[4 + comp]))
        staged.append(pltpu.make_async_copy(panel(comp, other), away.at[:, lanes_of[comp]], in_sem.at[6 + comp]))
    for copy in staged:
        copy.start()

    def centre(zi, zj):
        delta = (zj - zi) % NZ
        from_i = jnp.where(delta >= 2, 1, 0)
        from_j = jnp.where(delta == 7, 0, jnp.where(delta == 4, 2, 1))
        zc = jnp.where(delta <= 3, zi + from_i, zj + from_j) % NZ
        return delta, zc

    core_rows = pl.ds(pl.multiple_of(core * 16, 16), 16)

    def as_it_is(delta):
        return jnp.logical_or(delta == 0, delta >= 4)

    def pair_dest(plane, zl):
        delta, zc = centre(2 * x + zl, z)
        swap = as_it_is(delta)
        return delta, dev(plane, jnp.where(swap, yl, yh), jnp.where(swap, yh, yl), zc, core)

    pair_dests = []
    for plane in range(NX):
        for zl in range(2):
            pair_dests.append((plane, zl) + pair_dest(plane, zl))
    up = [dev(plane, yh, x // 2, z, core) for plane in range(NX)]
    down = [dev(2 * yl + k // 2, yh, k % 2, z, core) for k in range(4)]

    log_copy.wait()
    l_src[...] = jnp.zeros_like(l_src)
    for f in range(NX):
        l_src[f, :, 0:RUN] = log_v[0, f : f + 1, :]

    partner = dev(x, yh, other, z, core)
    diagonal = {d: dev(x, yh, other, (z + d) % NZ, core) for d in (1, -1)}
    y_near = [odev(dy, 0)[2] for dy in (1, 3)]
    across = dev(x, 1 - yh, other, z, core)
    sibling = dev(x, yh, yl, z, 1 - core)
    z_near = [zdev(d) for d in (1, -1, 2, -2)]
    xy_near = [dev((x + dx) % NX, yh, lo, z, core) for dx in (2, 1, 3) for lo in (other, yl)]
    near = xy_near + [diagonal[1], diagonal[-1], partner, across, sibling] + z_near
    barrier = pltpu.get_barrier_semaphore()
    for dest in near:
        pl.semaphore_signal(barrier, inc=1, device_id=dest, device_id_type=MESH)
    for copy in staged:
        copy.wait()
    pl.semaphore_wait(barrier, len(near))

    def pass_token(k, dests):
        for dest in dests:
            pl.semaphore_signal(tokens.at[k], inc=1, device_id=dest, device_id_type=MESH)


    def send(src, dst, s_sem, r_sem, dest):
        copy = pltpu.make_async_remote_copy(
            src_ref=src, dst_ref=dst, send_sem=s_sem, recv_sem=r_sem, device_id=dest, device_id_type=MESH
        )
        copy.start()
        return copy

    def send_or_keep(src, dst, s_sem, r_sem, dest):
        mine = is_me(dest)
        @pl.when(jnp.logical_not(mine))
        def _():
            send(src, dst, s_sem, r_sem, dest)
        @pl.when(mine)
        def _():
            pltpu.make_async_copy(src, dst, r_sem).start()

    def finish_send(src, s_sem, dest):
        @pl.when(jnp.logical_not(is_me(dest)))
        def _():
            wait_bytes(src, s_sem)

    slot = (x % 2) * 2 + yl
    for f in range(NX):
        send_or_keep(l_src.at[f], l_in.at[slot], ls_sem.at[f], lr_sem.at[0], up[f])

    def launch(k, comp, src, dst, dest):
        send(src, dst.at[:, lanes_of[comp]], gs_sem.at[comp, k], gr_sem.at[comp, k], dest)

    own = u.at[0, yl, 0]
    for comp in range(2):
        launch(1, comp, own.at[:, lanes_of[comp]], x_left.at[1, yl], zdev(1))
        launch(2, comp, own.at[:, lanes_of[comp]], u.at[1, yl, 0], zdev(-1))
        launch(0, comp, away.at[:, lanes_of[comp]], u.at[0, yl, 0], partner)
    for comp in range(2):
        launch(3, comp, away.at[:, lanes_of[comp]], x_left.at[1, yl], diagonal[1])
        launch(4, comp, away.at[:, lanes_of[comp]], u.at[1, yl, 0], diagonal[-1])

    def build_turned(lo, j):
        u[j, lo, 1, :, 0:NP] = -u[j, lo, 0, :, NP : 2 * NP]
        u[j, lo, 1, :, NP : 2 * NP] = u[j, lo, 0, :, 0:NP]

    def build_weighted(g, psd2):
        for lo in range(2):
            x_psd[g, lo] = (x_left[g, lo].astype(F32) * psd2).astype(BF16)

    def correlate(it, j):
        tiles = [k for k, pair in enumerate(PAIRS) if pair[1] == j]
        first = PAIRS[tiles[0]][0]
        left = x_psd[first : first + len(tiles)].reshape(len(tiles) * 2 * ST, 2 * NP)
        right = u[j].reshape(4 * ST, 2 * NP)
        product = lax.dot_general(left, right, (((1,), (1,)), ((), ())), preferred_element_type=F32)
        for k, tile in enumerate(tiles):
            block = product[k * 2 * ST : (k + 1) * 2 * ST].reshape(2, 2, 16, 128).astype(BF16)
            for half in range(2):
                c_part[it, half, tile] = block[:, half]

    def sum_sems(it, first, stage):
        k = stage if first == 0 else 5 + stage
        return ph_s.at[it, k], ph_r.at[it, k]

    def sum_tiles(it, first, last):
        tiles = pl.ds(first, last - first)
        s_sem, r_sem = sum_sems(it, first, 0)
        send(c_part.at[it, 1 - core, tiles], core_in.at[it, tiles], s_sem, r_sem, sibling)
        wait_bytes(core_in.at[it, tiles], r_sem)
        y_all[it, y_at, tiles] = (c_part[it, core, tiles].astype(F32) + core_in[it, tiles].astype(F32)).astype(BF16)
        s_sem, r_sem = sum_sems(it, first, 1)
        for dy in (2, 1, 3):
            send(y_all.at[it, y_at, tiles], y_all.at[it, y_at, tiles], s_sem, r_sem, odev(dy, 0)[2])

    def arrive(k, comp, dst):
        wait_bytes(dst.at[:, lanes_of[comp]], gr_sem.at[comp, k])

    def pass_on(half, at):
        for comp in range(2):
            piece = x_left.at[1, half]
            arrive(at, comp, piece)
            launch(at + 4, comp, piece.at[:, lanes_of[comp]], x_left.at[2, half], zdev(1))
            piece = u.at[1, half, 0]
            arrive(at + 1, comp, piece)
            launch(at + 5, comp, piece.at[:, lanes_of[comp]], u.at[2, half, 0], zdev(-1))

    pass_token(0, z_near)

    lane_at = lax.broadcasted_iota(jnp.int32, (ST, 128), 1)
    same = (lane_at % ST == lax.broadcasted_iota(jnp.int32, (ST, 128), 0)).astype(BF16)
    part_at = lane_at // ST

    def turned(block):
        full = lax.dot_general(block, same, (((0,), (0,)), ((), ())), preferred_element_type=F32)
        result = jnp.where(part_at == 0, full[0:ST], full[ST : 2 * ST])
        result = jnp.where(part_at == 2, full[2 * ST : 3 * ST], result)
        return jnp.where(part_at == 3, full[3 * ST : 4 * ST], result)

    obs_copy.wait()
    w_copy.wait()
    for zl in range(2):
        w = w_v[:, zl * ST : (zl + 1) * ST].astype(F32)
        for f in range(NX):
            real = w * obs_v[f, 0, :, zl * ST : (zl + 1) * ST]
            imag = w * obs_v[f, 1, :, zl * ST : (zl + 1) * ST]
            block = jnp.concatenate([real, imag, w, w], axis=1).astype(BF16)
            msg[f, zl] = jnp.where(as_it_is(pair_dests[zl][2]), block.astype(F32), turned(block)).astype(BF16)

    pl.semaphore_wait(tokens.at[0], len(z_near))
    pass_token(1, y_near)
    wait_bytes(l_in, lr_sem.at[0])
    for d in z_steps:
        send(l_in, l_z.at[z], ls2_sem.at[0], lr_sem.at[1], zdev(d))
    l_z[z] = l_in[...]
    pass_on(yl, 1)
    pass_on(other, 3)
    pl.semaphore_wait(tokens.at[1], len(y_near))
    for comp in range(2):
        arrive(0, comp, u.at[0, other, 0])
    for k, (plane, zl, delta, dest) in enumerate(pair_dests):
        send_or_keep(msg.at[plane, zl, core_rows], e_in.at[delta], es_sem.at[k], er_sem.at[0], dest)
    for lo in range(2):
        x_left[0, lo] = u[0, lo, 0]
        build_turned(lo, 0)
        build_turned(lo, 1)

    wait_bytes(l_z.at[pl.ds(0, NZ - 1)], lr_sem.at[1])
    for zz in range(NZ):
        for k in range(4):
            l_rows[k * NZ + zz : k * NZ + zz + 1, :] = l_z[zz, k]
    point = lax.broadcasted_iota(jnp.int32, (128, NP), 1)
    run_of = lax.shift_right_logical(point * 2731, 16)
    spread = (point - run_of * RUN == lax.broadcasted_iota(jnp.int32, (128, NP), 0)).astype(F32)
    spread_rows = jnp.dot(l_rows[...], spread, precision=HIGHEST, preferred_element_type=F32)
    run_row = lax.shift_right_logical(lax.broadcasted_iota(jnp.int32, (32, NP), 1) * 2731, 16)
    log_field = jnp.sum(
        jnp.where(run_row == lax.broadcasted_iota(jnp.int32, (32, NP), 0), spread_rows, 0.0), axis=0, keepdims=True
    )
    psd = jnp.exp(log_field)
    psd2 = jnp.concatenate([psd, psd], axis=1)
    build_weighted(0, psd2)

    build_weighted(1, psd2)
    correlate(0, 0)
    correlate(0, 1)
    sum_tiles(0, 0, 3)

    for half, at in ((yl, 5), (other, 7)):
        for comp in range(2):
            arrive(at, comp, x_left.at[2, half])
            arrive(at + 1, comp, u.at[2, half, 0])
    for lo in range(2):
        build_turned(lo, 2)
    build_weighted(2, psd2)
    correlate(0, 2)

    def pair_terms():
        wait_bytes(e_in, er_sem.at[0])
        part_at = lax.broadcasted_iota(jnp.int32, (16, 128), 1) // ST

        def conj(block):
            block = block.astype(F32)
            return jnp.where(part_at == 1, -block, block)

        blocks = (
            conj(e_in[0]),
            e_in[1].astype(F32) + conj(e_in[7]),
            e_in[2].astype(F32) + conj(e_in[6]),
            e_in[3].astype(F32) + conj(e_in[5]),
            conj(e_in[4]),
        )
        for tile, block in enumerate(blocks):
            pair_all[y_at, tile] = jnp.where(yl == 0, block, pltpu.roll(block, 64, 1)).astype(BF16)
        for dy in (2, 1, 3):
            send(pair_all.at[y_at], pair_all.at[y_at], pt_sem.at[0], pt_sem.at[1], odev(dy, 0)[2])

    def pair_tiles():
        wait_bytes(pair_all.at[pl.ds(0, 3)], pt_sem.at[1])
        low = lax.broadcasted_iota(jnp.int32, (16, 128), 1) < 64
        for tile in range(len(PAIRS)):
            for hi in range(2):
                first = pair_all[2 * hi, tile].astype(F32)
                second = pair_all[2 * hi + 1, tile].astype(F32)
                d_all[tile, hi] = jnp.where(low, first, second)
                w_all[tile, hi] = jnp.where(low, pltpu.roll(first, 64, 1), pltpu.roll(second, 64, 1)) * QUAD

    def finish_phase(it, phase):
        if phase == 2:
            wait_bytes(g_all.at[it, pl.ds(0, NZ - 1)], ph_s.at[it, 2])
        elif phase == 3:
            wait_bytes(s_all.at[it, pl.ds(0, NS - 1)], ph_s.at[it, 3])
        elif phase == 4:
            wait_bytes(core_in.at[it], ph_s.at[it, 4])
        else:
            for part in ((0, 3), (3, 5)) if it == 0 else ((0, 5),):
                tiles = pl.ds(part[0], part[1] - part[0])
                left = core_in.at[it, tiles] if phase == 0 else y_all.at[it, pl.ds(0, 3), tiles]
                wait_bytes(left, sum_sems(it, part[0], phase)[0])

    def finish_start():
        for comp in range(2):
            for k in range(9):
                wait_bytes(x_left.at[1, 0, :, lanes_of[comp]], gs_sem.at[comp, k])
        for f in range(NX):
            finish_send(l_src.at[f], ls_sem.at[f], up[f])
        wait_bytes(l_z.at[pl.ds(0, NZ - 1)], ls2_sem.at[0])
        for k, (plane, zl, delta, dest) in enumerate(pair_dests):
            finish_send(msg.at[plane, zl, core_rows], es_sem.at[k], dest)
        wait_bytes(pair_all.at[pl.ds(0, 3)], pt_sem.at[0])
        for phase in range(5):
            finish_phase(0, phase)

    def exchange_rest(it, psd):
        phase = lambda k: (ph_s.at[it, k], ph_r.at[it, k])
        sum_tiles(it, 3 if it == 0 else 0, 5)
        if it == 0:
            pair_terms()
            pair_tiles()
        else:
            finish_start()
        for part in ((0, 3), (3, 5)) if it == 0 else ((0, 5),):
            tiles = pl.ds(part[0], part[1] - part[0])
            wait_bytes(y_all.at[it, pl.ds(0, 3), tiles], sum_sems(it, part[0], 1)[1])
        total = y_all[it, 0].astype(F32)
        for k in range(1, 4):
            total = total + y_all[it, k].astype(F32)
        b_full[it, core] = (w_all[...] * total - d_all[...]).astype(BF16)
        s_sem, r_sem = phase(4)
        send(b_full.at[it, core], b_full.at[it, core], s_sem, r_sem, sibling)
        wait_bytes(core_in.at[it], r_sem)

        width = 384
        terms = []
        for c in range(2 * NP // width):
            lanes = slice(c * width, (c + 1) * width)
            term = jnp.zeros((1, width), F32)
            for g in range(3):
                tiles = [k for k, pair in enumerate(PAIRS) if pair[0] == g]
                first = PAIRS[tiles[0]][1]
                b = jnp.concatenate(
                    [
                        jnp.concatenate([b_full[it, half, tile, hi] for hi in range(2) for half in range(2)], axis=0)
                        for tile in tiles
                    ],
                    axis=1,
                )
                right = u[first : first + len(tiles), :, :, :, lanes].reshape(len(tiles) * 4 * ST, width)
                field = jnp.dot(b, right, preferred_element_type=F32)
                left = x_left[g, :, :, lanes].reshape(2 * ST, width).astype(F32)
                term = term + jnp.sum(left * field, axis=0, keepdims=True)
            terms.append(term)
        half = len(terms) // 2
        mine = jnp.concatenate([terms[k] + terms[half + k] for k in range(half)], axis=1)
        g_mine[it] = mine
        s_sem, r_sem = phase(2)
        for d in z_steps:
            send(g_mine.at[it], g_all.at[it, z], s_sem, r_sem, zdev(d))
        g_all[it, z] = mine
        wait_bytes(g_all.at[it, pl.ds(0, NZ - 1)], r_sem)
        summed = g_all[it, 0]
        for k in range(1, NZ):
            summed = summed + g_all[it, k]
        return QUAD * psd * summed

    def start_mean(it, gradient):
        squares = gradient[:, 0:128] * gradient[:, 0:128]
        for k in range(1, NP // 128):
            squares = squares + gradient[:, k * 128 : (k + 1) * 128] * gradient[:, k * 128 : (k + 1) * 128]
        s_mine[it] = squares
        for step in s_steps:
            send(s_mine.at[it], s_all.at[it, mine_at], ph_s.at[it, 3], ph_r.at[it, 3], sdev(*step))
        s_all[it, mine_at] = squares

    def finish_mean(it):
        wait_bytes(s_all.at[it, pl.ds(0, NS - 1)], ph_r.at[it, 3])
        total = jnp.sum(jnp.sum(s_all[it], axis=0), axis=1, keepdims=True)
        return jnp.sqrt(total / ENTRIES + EPSILON)

    gradient = exchange_rest(0, psd)
    start_mean(0, gradient)
    log_field = log_field - DESCENT * gradient / finish_mean(0)

    psd = jnp.exp(log_field)
    psd2 = jnp.concatenate([psd, psd], axis=1)
    for g in range(3):
        build_weighted(g, psd2)
    for j in range(3):
        correlate(1, j)
    m_mine[...] = log_field
    for k in range(4):
        send_or_keep(m_mine, m_in.at[x], ms_sem.at[k], mr_sem.at[0], down[k])
    gradient = exchange_rest(1, psd)
    start_mean(1, gradient)
    o_mine[...] = gradient
    for k in range(4):
        send_or_keep(o_mine, o_in.at[x], os_sem.at[k], or_sem.at[0], down[k])

    start = (slot * NZ + z) * RUN
    pick = (
        lax.broadcasted_iota(jnp.int32, (NP, 128), 0) == lax.broadcasted_iota(jnp.int32, (NP, 128), 1) + start
    ).astype(F32)

    def run_of_points(rows, parts):
        rows[...] = jnp.zeros_like(rows)
        for f in range(NX):
            rows[f : f + 1, :] = parts[f]
        return jnp.dot(rows[...], pick, precision=HIGHEST, preferred_element_type=F32)[0:NX, 0:RUN]

    wait_bytes(m_in, mr_sem.at[0])
    own_field = run_of_points(rows_m, m_in)
    wait_bytes(o_in, or_sem.at[0])
    own_gradient = run_of_points(rows_o, o_in)
    out[0] = own_field - DESCENT * own_gradient / finish_mean(1)

    for phase in range(5):
        finish_phase(1, phase)
    for k in range(4):
        finish_send(m_mine, ms_sem.at[k], down[k])
        finish_send(o_mine, os_sem.at[k], down[k])


def body(green_panel, log_psd, observed, pair_weights):
    vmem = pltpu.VMEM
    dma = pltpu.SemaphoreType.DMA
    return pl.pallas_call(
        kernel,
        out_shape=jax.ShapeDtypeStruct(log_psd.shape, F32),
        in_specs=[
            pl.BlockSpec(memory_space=pltpu.HBM),
            pl.BlockSpec(memory_space=pltpu.HBM),
            pl.BlockSpec(memory_space=pltpu.HBM),
            pl.BlockSpec(memory_space=pltpu.HBM),
        ],
        out_specs=pl.BlockSpec(memory_space=pltpu.VMEM),
        scratch_shapes=[
            vmem((3, 2, 2, ST, 2 * NP), BF16),
            vmem((3, 2, ST, 2 * NP), BF16),
            vmem((3, 2, ST, 2 * NP), BF16),
            vmem((ST, 2 * NP), BF16),
            vmem((1, NX, RUN), F32),
            vmem((NX, 2, ST, 2 * ST), F32),
            vmem((ST, 2 * ST), jnp.int32),
            vmem((NX, 2, ST, 128), BF16),
            vmem((NZ, 16, 128), BF16),
            vmem((5, 2, 16, 128), F32),
            vmem((5, 2, 16, 128), F32),
            vmem((NX, 1, 128), F32),
            vmem((4, 1, 128), F32),
            vmem((NZ, 4, 1, 128), F32),
            vmem((32, 128), F32),
            vmem((4, 5, 16, 128), BF16),
            vmem((ITERS, 2, 5, 2, 16, 128), BF16),
            vmem((ITERS, 5, 2, 16, 128), BF16),
            vmem((ITERS, 4, 5, 2, 16, 128), BF16),
            vmem((ITERS, 2, 5, 2, 16, 128), BF16),
            vmem((ITERS, 1, NP), F32),
            vmem((ITERS, NZ, 1, NP), F32),
            vmem((ITERS, 1, 128), F32),
            vmem((ITERS, NS, 1, 128), F32),
            vmem((1, NP), F32),
            vmem((1, NP), F32),
            vmem((NX, 1, NP), F32),
            vmem((NX, 1, NP), F32),
            vmem((8, NP), F32),
            vmem((8, NP), F32),
            dma((8,)),
            dma((2, 9)),
            dma((2, 9)),
            dma((1,)),
            dma((8,)),
            dma((2,)),
            dma((4,)),
            dma((1,)),
            pltpu.SemaphoreType.REGULAR((2,)),
            dma((2,)),
            dma((ITERS, 7)),
            dma((ITERS, 7)),
            dma((1,)),
            dma((4,)),
            dma((1,)),
            dma((4,)),
        ],
        compiler_params=pltpu.CompilerParams(
            collective_id=0, has_side_effects=True, vmem_limit_bytes=63 * 1024 * 1024
        ),
    )(green_panel, log_psd, jnp.swapaxes(observed, 2, 3), pair_weights.T)


def solution(mesh):
    return jax.shard_map(
        body,
        mesh=mesh,
        in_specs=(
            P(None, None, "col", "pts"),
            P("pts", None, ("row", "col")),
            P(None, None, "row", "col"),
            P("row", "col"),
        ),
        out_specs=P("pts", None, ("row", "col")),
        check_vma=False,
    )
```
